32 devices in a mesh: req: 32 (over z, y, x, core), mlp: 1.
Axes of the slice: x: 2, y: 2, z: 4, core: 2. Of those that a mesh axis runs over, the one named last changes fastest.
Arguments:
- queries: bfloat16 [8192, 8, 256], P('req', 'mlp'), may hold values from -7 to 7
- new_kv: bfloat16 [8192, 8, 512], P('req', 'mlp'), may hold values from -6 to 6
- cache_pool: bfloat16 [192, 128, 8, 512], P('req', None, 'mlp'), may hold values from -6 to 6
- page_table: int32 [32, 6], P('req'), may hold values from 0 to 5, each once within a row
- assignment: int32 [32], P('req'), may hold values from 0 to 31, each once
- lengths: int32 [32], replicated, may hold values from 1 to 768, 6144 in all
- lambda_vectors: float32 [4, 128], replicated, may hold values from -0.4 to 0.4
- subln_gain: float32 [256], replicated, may hold values from 0.5 to 1.5
- residual: bfloat16 [8192, 2048], P('req', 'mlp'), may hold values from -70 to 70
- out_weight: bfloat16 [2048, 2048], P('req', 'mlp'), may hold values from -0.125 to 0.125
- norm_gain: float32 [2048], replicated, may hold values from 0.5 to 1.5
- gate_weight: bfloat16 [2048, 3072], P('req', 'mlp'), may hold values from -0.125 to 0.125
- up_weight: bfloat16 [2048, 3072], P('req', 'mlp'), may hold values from -0.125 to 0.125
- down_weight_t: bfloat16 [2048, 3072], P('req', 'mlp'), may hold values from -0.109375 to 0.109375
Outputs:
- layer_out: bfloat16 [8192, 2048], P('req', 'mlp')
The draws below stay inside these ranges and needn't reach their ends.
Inputs may be any that keep to these rules, and one draw needn't show every extreme that they name: `page_table`: row g lists the cache pages of slot g in logical order as offsets from page g * 6; each offset once in a row. `assignment`: every request is served by exactly one slot. `lengths`: indexed by request; some request has exactly 768 cached tokens.
All inputs are finite; a program needn't handle non-finite values.
Results may differ from the reference program's by a relative error of at most 0.011.
Values may be sent and summed in bfloat16 or wider, within the bound.
A program may use at most 128 MiB of HBM per device.

```python
import math
import jax
import jax.numpy as jnp
import numpy as np
from jax import lax

D = 2048
HEADS = 8
HALF = 128
FFW = 3072
PAGE = 128
MAXP = 6
NEW = 256
REQS = 32
TOKENS = 8192
POOL = 192
N_MLP = 1


def draw_queries(key, part):
    values = jnp.clip(jax.random.normal(jax.random.fold_in(key, 11), (TOKENS, HEADS, 2 * HALF), jnp.float32), -6.0, 6.0)
    return values.astype(jnp.bfloat16)


def draw_new_kv(key, part):
    values = jnp.clip(jax.random.normal(jax.random.fold_in(key, 12), (TOKENS, HEADS, 4 * HALF), jnp.float32), -6.0, 6.0)
    return values.astype(jnp.bfloat16)


def draw_residual(key, part):
    row_key = jax.random.fold_in(key, 21)
    col_key = jax.random.fold_in(key, 22)
    val_key = jax.random.fold_in(key, 23)
    columns = jnp.arange(D, dtype=jnp.float32) / D
    col_scale = 0.3 * 10.0 ** (columns + 0.2 * jax.random.uniform(col_key, (D,), jnp.float32) - 0.1)
    row_scale = 10.0 ** (jax.random.uniform(row_key, (TOKENS, 1), jnp.float32) - 0.5)
    values = jnp.clip(jax.random.normal(val_key, (TOKENS, D), jnp.float32), -6.0, 6.0)
    return (values * col_scale * row_scale).astype(jnp.bfloat16)


def block_scale(stream_key, dims, shards, least, largest):
    def one(axis_at, blocks):
        draws = jax.random.uniform(jax.random.fold_in(jax.random.fold_in(stream_key, 6), axis_at), (blocks,), jnp.float32, least / len(shards), largest / len(shards))
        return jnp.repeat(jnp.exp(draws), dims[axis_at] // blocks).reshape((-1,) + (1,) * (len(dims) - axis_at - 1))

    gain = one(*shards[0])
    for cut in shards[1:]:
        gain = gain * one(*cut)
    return gain


def split_up(amount, total, reach, lean):
    loads = [(1 << 20) // math.isqrt(standing ** lean) + 1 for standing in range(2, amount + 1)]
    spare, holding = total - reach - (amount - 1), [1] * (amount - 1)
    while spare > 0:
        candidates = [i for i in range(amount - 1) if holding[i] < reach]
        mass, remaining = sum([loads[i] for i in candidates]), spare
        for i in candidates:
            addition = min(reach - holding[i], max(1, remaining * loads[i] // mass), spare)
            holding[i] = holding[i] + addition
            spare = spare - addition
    return np.array([reach] + holding)


def ragged(own_key, number_of, total, reach, slope):
    if number_of == 2:
        one = jax.random.randint(own_key, (), max(1, total - reach), min(reach, total - 1) + 1)
        return jnp.stack([one, total - one])
    sizes = jnp.asarray(split_up(number_of, total, reach, slope), jnp.int32)
    couples = (number_of - 1) // 2
    donor, sink = sizes[1:1 + 2 * couples:2], sizes[2:2 + 2 * couples:2]
    margin = jnp.minimum(donor - 1, reach - sink)
    passed = jax.random.randint(jax.random.fold_in(own_key, 1), (couples,), 0, 1 << 20) % (margin + 1)
    sizes = sizes.at[1:1 + 2 * couples:2].set(donor - passed).at[2:2 + 2 * couples:2].set(sink + passed)
    return sizes[jax.random.permutation(jax.random.fold_in(own_key, 2), number_of)]


def scatter_about(stream_key, shape, width, limit, split=(), kind=jnp.bfloat16):
    factor_of = block_scale(stream_key, shape, split, -0.22, 0.18) if split else 1.0
    entries = jax.random.normal(stream_key, shape, jnp.float32) * width * factor_of
    return jnp.minimum(jnp.maximum(entries, -limit), limit).astype(kind)


def setup_inputs(seed: int = 0) -> dict:
    key_of = jax.random.split(jax.random.key(seed), 15)
    return {
        "queries": draw_queries(jax.random.fold_in(key_of[14], 71), 0),
        "new_kv": draw_new_kv(jax.random.fold_in(key_of[14], 71), 0),
        "cache_pool": scatter_about(key_of[2], (POOL, PAGE, HEADS, 4 * HALF), 1.0, 6.0, ((0, 32),)),
        "page_table": jax.vmap(lambda own: jax.random.permutation(own, MAXP))(jax.random.split(key_of[3], REQS)).reshape((REQS, MAXP)).astype(jnp.int32),
        "assignment": jax.random.permutation(key_of[4], REQS).astype(jnp.int32),
        "lengths": ragged(key_of[5], REQS, REQS * MAXP * PAGE // 4, MAXP * PAGE, 2).astype(jnp.int32),
        "lambda_vectors": scatter_about(key_of[6], (4, HALF), 0.1, 0.4, (), jnp.float32),
        "subln_gain": jnp.clip(1.0 + 0.1 * jax.random.normal(key_of[7], (2 * HALF,), jnp.float32), 0.5, 1.5),
        "residual": draw_residual(jax.random.fold_in(key_of[14], 71), 0),
        "out_weight": scatter_about(key_of[9], (2 * HEADS * HALF, D), (2 * HEADS * HALF) ** -0.5, 0.125, ((0, 32),)),
        "norm_gain": jnp.clip(1.0 + 0.1 * jax.random.normal(key_of[10], (D,), jnp.float32), 0.5, 1.5),
        "gate_weight": scatter_about(key_of[11], (D, FFW), D ** -0.5, 0.125, ((0, 32),)),
        "up_weight": scatter_about(key_of[12], (D, FFW), D ** -0.5, 0.125, ((0, 32),)),
        "down_weight_t": scatter_about(key_of[13], (D, FFW), FFW ** -0.5, 0.109375, ((0, 32),)),
    }


NEG_FILL = -1e+30
LAMBDA_BASE = 0.2

def one_map(query_rows, key_half, value_rows, visible):
    score = jnp.einsum('nhd,khd->nhk', query_rows.astype(jnp.float32), key_half.astype(jnp.float32)) * HALF ** (-0.5)
    score = jnp.where(visible[:, None, :], score, NEG_FILL)
    row_max = lax.optimization_barrier(jnp.max(score, axis=2, keepdims=True))
    exp_terms = jnp.where(visible[:, None, :], jnp.exp(score - row_max), 0.0)
    exp_total = lax.optimization_barrier(jnp.sum(exp_terms, axis=2))
    rounded = lax.optimization_barrier(exp_terms.astype(jnp.bfloat16))
    mixed_vals = jnp.einsum('nhk,khd->nhd', rounded.astype(jnp.float32), value_rows.astype(jnp.float32))
    return mixed_vals / exp_total[:, :, None]

def reference(queries, new_kv, cache_pool, page_table, assignment, lengths, lambda_vectors, subln_gain, residual, out_weight, norm_gain, gate_weight, up_weight, down_weight_t):
    lambda_now = jnp.exp(jnp.sum(lambda_vectors[0] * lambda_vectors[1])) - jnp.exp(jnp.sum(lambda_vectors[2] * lambda_vectors[3])) + LAMBDA_BASE
    cache_len = MAXP * PAGE
    group_size = FFW // N_MLP

    def one_slot(slot_index):
        row_start = slot_index * NEW
        q_rows = lax.dynamic_slice_in_dim(queries, row_start, NEW, 0)
        kv_rows = lax.dynamic_slice_in_dim(new_kv, row_start, NEW, 0)
        slot_pages = lax.dynamic_slice_in_dim(cache_pool, slot_index * MAXP, MAXP, 0)
        table_row = lax.dynamic_index_in_dim(page_table, slot_index, 0, keepdims=False)
        cached = lengths[assignment[slot_index]]
        cached_rows = slot_pages[table_row].reshape(cache_len, HEADS, 4 * HALF)
        key_rows = jnp.concatenate([cached_rows, kv_rows], axis=0)
        positions = jnp.arange(cache_len, dtype=jnp.int32)
        token_pos = jnp.arange(NEW, dtype=jnp.int32)
        visible = jnp.concatenate([jnp.broadcast_to((positions < cached)[None, :], (NEW, cache_len)), token_pos[None, :] <= token_pos[:, None]], axis=1)
        value_rows = key_rows[:, :, 2 * HALF:]
        map_one = one_map(q_rows[:, :, :HALF], key_rows[:, :, :HALF], value_rows, visible)
        map_two = one_map(q_rows[:, :, HALF:], key_rows[:, :, HALF:2 * HALF], value_rows, visible)
        mix_out = map_one - lambda_now * map_two
        mix_out = mix_out * lax.rsqrt(lax.optimization_barrier(jnp.mean(mix_out * mix_out, axis=2, keepdims=True)) + 1e-05) * subln_gain * (1.0 - LAMBDA_BASE)
        attn_out = mix_out.astype(jnp.bfloat16).reshape(NEW, HEADS * 2 * HALF)
        x_rows = lax.dynamic_slice_in_dim(residual, row_start, NEW, 0)
        stream = (x_rows.astype(jnp.float32) + jnp.dot(attn_out, out_weight, preferred_element_type=jnp.float32)).astype(jnp.bfloat16)
        stream_f = lax.optimization_barrier(stream).astype(jnp.float32)
        normed = (stream_f * lax.rsqrt(lax.optimization_barrier(jnp.mean(stream_f * stream_f, axis=1, keepdims=True)) + 1e-05) * norm_gain).astype(jnp.bfloat16)
        gate_value = jnp.dot(normed, gate_weight, preferred_element_type=jnp.float32)
        up_value = jnp.dot(normed, up_weight, preferred_element_type=jnp.float32)
        hidden_act = (jax.nn.silu(gate_value) * up_value).astype(jnp.bfloat16)
        down_sum = jnp.zeros((NEW, D), jnp.float32)
        for group_index in range(N_MLP):
            group_lo = group_index * group_size
            group_hi = group_lo + group_size
            group_part = lax.dot_general(hidden_act[:, group_lo:group_hi], down_weight_t[:, group_lo:group_hi], (((1,), (1,)), ((), ())), preferred_element_type=jnp.float32)
            down_sum = down_sum + lax.optimization_barrier(group_part.astype(jnp.bfloat16)).astype(jnp.float32)
        return (stream_f + down_sum).astype(jnp.bfloat16)
    outputs = lax.map(one_slot, jnp.arange(REQS, dtype=jnp.int32))
    return outputs.reshape(TOKENS, D)
```

```python
import jax
import jax.numpy as jnp
from jax import lax
from jax.sharding import PartitionSpec as P

D = 2048


NEG_FILL = -1e30
LAMBDA_BASE = 0.2


def map_block(carried, query_rows, key_half, value_rows, visible, score_scale):
    running_max, running_sum, running_acc = carried
    score = (
        jnp.einsum("nhd,khd->nhk", query_rows, key_half, preferred_element_type=jnp.float32)
        * score_scale
    )
    score = jnp.where(visible[:, None, :], score, NEG_FILL)
    newest = jnp.maximum(running_max, jnp.max(score, axis=2))
    exp_terms = jnp.where(visible[:, None, :], jnp.exp(score - newest[:, :, None]), 0.0)
    shrink = jnp.exp(running_max - newest)
    running_sum = running_sum * shrink + jnp.sum(exp_terms, axis=2)
    running_acc = running_acc * shrink[:, :, None] + jnp.einsum(
        "nhk,khd->nhd",
        exp_terms.astype(jnp.bfloat16),
        value_rows,
        preferred_element_type=jnp.float32,
    )
    return (newest, running_sum, running_acc)


def both_maps(carried, query_rows, key_rows, visible, half_size):
    score_scale = half_size ** (-0.5)
    value_rows = key_rows[:, :, 2 * half_size :]
    map_one = map_block(
        carried[0],
        query_rows[:, :, :half_size],
        key_rows[:, :, :half_size],
        value_rows,
        visible,
        score_scale,
    )
    map_two = map_block(
        carried[1],
        query_rows[:, :, half_size:],
        key_rows[:, :, half_size : 2 * half_size],
        value_rows,
        visible,
        score_scale,
    )
    return (map_one, map_two)


def attend(
    queries, new_kv, cache_pool, page_table, assignment, lengths, lambda_vectors, subln_gain
):
    row_count, head_count, value_width = queries.shape
    half_size = value_width // 2
    page_len = cache_pool.shape[1]
    request = assignment[0]
    cached = jnp.sum(
        jnp.where(jnp.arange(lengths.shape[0], dtype=jnp.int32) == request, lengths, 0)
    )

    def fresh_state():
        return (
            jnp.full((row_count, head_count), NEG_FILL, jnp.float32),
            jnp.zeros((row_count, head_count), jnp.float32),
            jnp.zeros((row_count, head_count, value_width), jnp.float32),
        )

    table_row = page_table[0]

    def page_step(page_index, carried):
        physical = table_row[page_index]
        page_rows = lax.dynamic_index_in_dim(cache_pool, physical, 0, keepdims=False)
        positions = page_index * page_len + jnp.arange(page_len, dtype=jnp.int32)
        visible = jnp.broadcast_to((positions < cached)[None, :], (row_count, page_len))
        return both_maps(carried, queries, page_rows, visible, half_size)

    page_count = (cached + page_len - 1) // page_len
    carried = lax.fori_loop(jnp.int32(0), page_count, page_step, (fresh_state(), fresh_state()))
    token_pos = jnp.arange(row_count, dtype=jnp.int32)
    carried = both_maps(
        carried, queries, new_kv, token_pos[None, :] <= token_pos[:, None], half_size
    )
    lambda_now = (
        jnp.exp(jnp.sum(lambda_vectors[0] * lambda_vectors[1]))
        - jnp.exp(jnp.sum(lambda_vectors[2] * lambda_vectors[3]))
        + LAMBDA_BASE
    )
    mix_out = (
        carried[0][2] / carried[0][1][:, :, None]
        - lambda_now * carried[1][2] / carried[1][1][:, :, None]
    )
    mix_out = (
        mix_out
        * lax.rsqrt(jnp.mean(mix_out * mix_out, axis=2, keepdims=True) + 1e-05)
        * subln_gain
        * (1.0 - LAMBDA_BASE)
    )
    return mix_out.astype(jnp.bfloat16).reshape(row_count, head_count * value_width)


def per_device(
    queries,
    new_kv,
    cache_pool,
    page_table,
    assignment,
    lengths,
    lambda_vectors,
    subln_gain,
    residual,
    out_weight,
    norm_gain,
    gate_weight,
    up_weight,
    down_weight_t,
):
    attn_out = attend(
        queries, new_kv, cache_pool, page_table, assignment, lengths, lambda_vectors, subln_gain
    )
    size = lax.axis_size("req")
    group = 4
    near = [[g * group + i for i in range(group)] for g in range(size // group)]
    far = [[g * group + i for g in range(size // group)] for i in range(group)]

    def own_columns(weight):
        rows, cols = weight.shape
        parts = jnp.swapaxes(weight.reshape(rows, group, cols // group), 0, 1)
        parts = lax.all_to_all(parts, "req", 0, 0, axis_index_groups=near)
        return parts.reshape(group * rows, cols // group)

    heads_all = lax.all_gather(attn_out, "mlp", axis=1, tiled=True)
    projected = jnp.dot(
        heads_all,
        lax.all_gather(out_weight, "req", axis=0, tiled=True),
        preferred_element_type=jnp.float32,
    )
    gathered = [
        lax.all_gather(own_columns(w), "req", axis=0, tiled=True, axis_index_groups=far)
        for w in (gate_weight, up_weight, down_weight_t)
    ]
    stream = (residual.astype(jnp.float32) + projected).astype(jnp.bfloat16)
    stream_f = stream.astype(jnp.float32)
    squares = lax.psum(jnp.sum(stream_f * stream_f, axis=1), "mlp")
    slice_width = stream_f.shape[1]
    local_gain = lax.dynamic_slice_in_dim(
        norm_gain, lax.axis_index("mlp") * slice_width, slice_width
    )
    normed_part = (stream_f * lax.rsqrt(squares / D + 1e-05)[:, None] * local_gain).astype(
        jnp.bfloat16
    )
    normed = lax.all_gather(normed_part, "mlp", axis=1, tiled=True)
    normed = lax.all_gather(normed, "req", axis=0, tiled=True, axis_index_groups=near)
    gate_value = jnp.dot(normed, gathered[0], preferred_element_type=jnp.float32)
    up_value = jnp.dot(normed, gathered[1], preferred_element_type=jnp.float32)
    hidden_act = (jax.nn.silu(gate_value) * up_value).astype(jnp.bfloat16)
    partial_value = lax.dot_general(
        hidden_act, gathered[2], (((1,), (1,)), ((), ())), preferred_element_type=jnp.float32
    ).astype(jnp.bfloat16)
    rows = stream.shape[0]
    pieces = lax.all_to_all(
        partial_value.reshape(group, rows, -1), "req", 0, 0, axis_index_groups=near
    )
    summed = lax.psum_scatter(
        jnp.sum(pieces.astype(jnp.float32), axis=0).astype(jnp.bfloat16),
        "mlp", scatter_dimension=1, tiled=True,
    ).astype(jnp.float32)
    return (stream_f + summed).astype(jnp.bfloat16)


def solution(mesh):
    in_specs = (
        P("req", "mlp", None),
        P("req", "mlp", None),
        P("req", None, "mlp", None),
        P("req", None),
        P("req"),
        P(),
        P(),
        P(),
        P("req", "mlp"),
        P("req", "mlp"),
        P(),
        P("req", "mlp"),
        P("req", "mlp"),
        P("req", "mlp"),
    )
    out_specs = P("req", "mlp")
    return jax.shard_map(
        per_device, mesh=mesh, in_specs=in_specs, out_specs=out_specs, check_vma=False
    )
```

```python
import jax
import jax.numpy as jnp
from jax import lax
from jax.experimental import pallas as pl
from jax.experimental.pallas import tpu as pltpu
from jax.sharding import PartitionSpec as P

D = 2048


NEG_FILL = -1e30
LAMBDA_BASE = 0.2


def map_block(carried, query_rows, key_half, value_rows, visible, score_scale):
    running_max, running_sum, running_acc = carried
    score = (
        jnp.einsum("nhd,khd->nhk", query_rows, key_half, preferred_element_type=jnp.float32)
        * score_scale
    )
    score = jnp.where(visible[:, None, :], score, NEG_FILL)
    newest = jnp.maximum(running_max, jnp.max(score, axis=2))
    exp_terms = jnp.where(visible[:, None, :], jnp.exp(score - newest[:, :, None]), 0.0)
    shrink = jnp.exp(running_max - newest)
    running_sum = running_sum * shrink + jnp.sum(exp_terms, axis=2)
    running_acc = running_acc * shrink[:, :, None] + jnp.einsum(
        "nhk,khd->nhd",
        exp_terms.astype(jnp.bfloat16),
        value_rows,
        preferred_element_type=jnp.float32,
    )
    return (newest, running_sum, running_acc)


def both_maps(carried, query_rows, key_rows, visible, half_size):
    score_scale = half_size ** (-0.5)
    value_rows = key_rows[:, :, 2 * half_size :]
    map_one = map_block(
        carried[0],
        query_rows[:, :, :half_size],
        key_rows[:, :, :half_size],
        value_rows,
        visible,
        score_scale,
    )
    map_two = map_block(
        carried[1],
        query_rows[:, :, half_size:],
        key_rows[:, :, half_size : 2 * half_size],
        value_rows,
        visible,
        score_scale,
    )
    return (map_one, map_two)


def attend(
    queries, new_kv, cache_pool, page_table, assignment, lengths, lambda_vectors, subln_gain
):
    row_count, head_count, value_width = queries.shape
    half_size = value_width // 2
    page_len = cache_pool.shape[1]
    request = assignment[0]
    cached = jnp.sum(
        jnp.where(jnp.arange(lengths.shape[0], dtype=jnp.int32) == request, lengths, 0)
    )

    def fresh_state():
        return (
            jnp.full((row_count, head_count), NEG_FILL, jnp.float32),
            jnp.zeros((row_count, head_count), jnp.float32),
            jnp.zeros((row_count, head_count, value_width), jnp.float32),
        )

    table_row = page_table[0]

    def page_step(page_index, carried):
        physical = table_row[page_index]
        page_rows = lax.dynamic_index_in_dim(cache_pool, physical, 0, keepdims=False)
        positions = page_index * page_len + jnp.arange(page_len, dtype=jnp.int32)
        visible = jnp.broadcast_to((positions < cached)[None, :], (row_count, page_len))
        return both_maps(carried, queries, page_rows, visible, half_size)

    page_count = (cached + page_len - 1) // page_len
    carried = lax.fori_loop(jnp.int32(0), page_count, page_step, (fresh_state(), fresh_state()))
    token_pos = jnp.arange(row_count, dtype=jnp.int32)
    carried = both_maps(
        carried, queries, new_kv, token_pos[None, :] <= token_pos[:, None], half_size
    )
    lambda_now = (
        jnp.exp(jnp.sum(lambda_vectors[0] * lambda_vectors[1]))
        - jnp.exp(jnp.sum(lambda_vectors[2] * lambda_vectors[3]))
        + LAMBDA_BASE
    )
    mix_out = (
        carried[0][2] / carried[0][1][:, :, None]
        - lambda_now * carried[1][2] / carried[1][1][:, :, None]
    )
    mix_out = (
        mix_out
        * lax.rsqrt(jnp.mean(mix_out * mix_out, axis=2, keepdims=True) + 1e-05)
        * subln_gain
        * (1.0 - LAMBDA_BASE)
    )
    return mix_out.astype(jnp.bfloat16).reshape(row_count, head_count * value_width)


def per_device(
    queries,
    new_kv,
    cache_pool,
    page_table,
    assignment,
    lengths,
    lambda_vectors,
    subln_gain,
    residual,
    out_weight,
    norm_gain,
    gate_weight,
    up_weight,
    down_weight_t,
):
    attn_out = attend(
        queries, new_kv, cache_pool, page_table, assignment, lengths, lambda_vectors, subln_gain
    )
    heads_all = lax.all_gather(attn_out, "mlp", axis=1, tiled=True)
    columns = heads_all
    projected = jnp.dot(
        columns,
        lax.all_gather(out_weight, "req", axis=0, tiled=True),
        preferred_element_type=jnp.float32,
    )
    stream = (residual.astype(jnp.float32) + projected).astype(jnp.bfloat16)
    stream_f = stream.astype(jnp.float32)
    squares = lax.psum(jnp.sum(stream_f * stream_f, axis=1), "mlp")
    slice_width = stream_f.shape[1]
    local_gain = lax.dynamic_slice_in_dim(
        norm_gain, lax.axis_index("mlp") * slice_width, slice_width
    )
    normed_part = (stream_f * lax.rsqrt(squares / D + 1e-05)[:, None] * local_gain).astype(
        jnp.bfloat16
    )
    normed = lax.all_gather(normed_part, "mlp", axis=1, tiled=True)
    columns = normed
    gate_value = jnp.dot(
        columns,
        lax.all_gather(gate_weight, "req", axis=0, tiled=True),
        preferred_element_type=jnp.float32,
    )
    up_value = jnp.dot(
        columns,
        lax.all_gather(up_weight, "req", axis=0, tiled=True),
        preferred_element_type=jnp.float32,
    )
    hidden_act = (jax.nn.silu(gate_value) * up_value).astype(jnp.bfloat16)
    partial_value = lax.dot_general(
        hidden_act,
        lax.all_gather(down_weight_t, "req", axis=0, tiled=True),
        (((1,), (1,)), ((), ())),
        preferred_element_type=jnp.float32,
    )
    summed = lax.psum_scatter(
        partial_value.astype(jnp.bfloat16), "mlp", scatter_dimension=1, tiled=True
    ).astype(jnp.float32)
    return (stream_f + summed).astype(jnp.bfloat16)


BF16, F32 = jnp.bfloat16, jnp.float32
MESH = pl.DeviceIdType.MESH


def layer_kernel(
    scale_ref, bias_ref, gain_ref, norm_ref, residual_ref,
    q_hbm, kv_hbm, out_hbm, gate_hbm, up_hbm, down_hbm,
    result_ref,
    q_buf, kv_buf, attn, wo, wg, wu, wd, normed, stream, hidden, part, got_core, to_x, got_x,
    load_sem, own_sem, first_send, first_recv, far_send, far_recv, o_send, o_recv,
    n_send, n_recv, d_send, d_recv,
):
    heads = q_buf.shape[0]
    rows = q_buf.shape[1]
    wide = q_buf.shape[2]
    half = wide // 2
    width = stream.shape[1]
    units = wg.shape[2]
    shard = out_hbm.shape[0]
    halfw = width // 2

    me = lax.axis_index("req")
    core = me % 2
    x = (me // 2) % 2
    quarter = me % 4
    y = (me // 4) % 2
    z = me // 8
    base = me - quarter
    side = z // 2
    inner = z + side * (3 - 2 * z)
    q_core = quarter + 1 - 2 * core
    q_x = (quarter + 2) % 4
    q_diag = (q_core + 2) % 4
    at_core, at_x, at_diag = base + q_core, base + q_x, base + q_diag
    at_y = me + 4 - 8 * y
    off = me - 8 * z
    at_n = off + 8 * (1 + side)
    at_e = off + 8 * (3 * side)
    at_m = off + 8 * (2 - side)
    is_end = inner == 0
    is_mid = inner == 1

    def order(k):
        o = k + inner * (1 - 2 * k) * (1 - k // 2)
        return o + side * (3 - 2 * o)

    def send(src, dst, ssem, rsem, device):
        return pltpu.make_async_remote_copy(
            src_ref=src, dst_ref=dst, send_sem=ssem, recv_sem=rsem,
            device_id={"req": device}, device_id_type=MESH,
        )

    barrier = pltpu.get_barrier_semaphore()

    def greet(device):
        pl.semaphore_signal(barrier, inc=1, device_id={"req": device}, device_id_type=MESH)

    for device in (at_core, at_x, at_diag, at_y):
        greet(device)

    @pl.when(is_end)
    def _():
        greet(at_n)
        pl.semaphore_wait(barrier, 5)

    @pl.when(is_mid)
    def _():
        greet(at_e)
        greet(at_m)
        pl.semaphore_wait(barrier, 6)

    my_half = pl.ds(pl.multiple_of(core * halfw, 128), halfw)
    other_half = pl.ds(pl.multiple_of((1 - core) * halfw, 128), halfw)
    my_rows = pl.ds(pl.multiple_of(quarter * shard, 64), shard)
    core_rows = pl.ds(pl.multiple_of(q_core * shard, 64), shard)
    x_rows = pl.ds(pl.multiple_of(x * 2 * shard, 128), 2 * shard)
    other_x_rows = pl.ds(pl.multiple_of((1 - x) * 2 * shard, 128), 2 * shard)

    o_own = pltpu.make_async_copy(out_hbm.at[:, my_half], wo.at[z, y, my_rows, my_half], own_sem.at[0])
    o_own.start()
    o_core = send(
        out_hbm.at[:, other_half], wo.at[z, y, my_rows, other_half], o_send.at[0], o_recv.at[0], at_core
    )
    o_core.start()

    firsts = []
    owns = []
    for m, (src, dst) in enumerate(((gate_hbm, wg), (up_hbm, wu), (down_hbm, wd))):
        block = dst.at[z * 2 + y, my_rows]
        mine = pltpu.make_async_copy(
            src.at[:, pl.ds(pl.multiple_of(quarter * units, 128), units)], block, own_sem.at[1 + m]
        )
        mine.start()
        owns.append(mine)
        group = []
        for k, (q_to, device) in enumerate(((q_core, at_core), (q_x, at_x), (q_diag, at_diag))):
            copy = send(
                src.at[:, pl.ds(pl.multiple_of(q_to * units, 128), units)],
                block, first_send.at[m, k], first_recv.at[m, k], device,
            )
            copy.start()
            group.append(copy)
        firsts.append(group)

    def load(h):
        return (
            pltpu.make_async_copy(q_hbm.at[h], q_buf.at[h], load_sem.at[0, h]),
            pltpu.make_async_copy(kv_hbm.at[h], kv_buf.at[h], load_sem.at[1, h]),
        )

    def start_load(h, carry):
        for copy in load(h):
            copy.start()
        return carry

    lax.fori_loop(0, heads, start_load, 0)

    mats = (wg, wu, wd)

    def along_z(block_at, send_sems, recv_sems, k):
        block = block_at(order(k))

        def to_end(slot):
            return send(block, block, send_sems(slot), recv_sems(slot), at_e)

        def to_mid(slot, at):
            return send(block, block, send_sems(at), recv_sems(slot), at_m)

        if k == 0:
            return (
                [send(block, block, send_sems(1), recv_sems(1), at_n)],
                [to_end(1), to_mid(2, 4)],
            )
        if k == 1:
            return [], [to_mid(3, 5)]
        return [], [to_end(k)]

    def z_start(copies):
        for_end, for_mid = copies
        if for_end:
            @pl.when(is_end)
            def _():
                for copy in for_end:
                    copy.start()

        @pl.when(is_mid)
        def _():
            for copy in for_mid:
                copy.start()

    def z_wait_send(copies):
        for_end, for_mid = copies
        if for_end:
            @pl.when(is_end)
            def _():
                for copy in for_end:
                    copy.wait_send()

        @pl.when(is_mid)
        def _():
            for copy in for_mid:
                copy.wait_send()

    def f_block(m):
        return lambda zz: mats[m].at[zz * 2 + y]

    def f_z(m, k):
        return along_z(
            f_block(m), lambda i: far_send.at[m, i], lambda i: far_recv.at[m, i], k
        )

    def f_z_recv(m, k):
        block = f_block(m)(order(k))
        send(block, block, far_send.at[m, k], far_recv.at[m, k], at_y).wait_recv()

    def f_y(m, k):
        block = f_block(m)(order(k))
        return send(block, block, far_send.at[m, 6 + k], far_recv.at[m, 6 + k], at_y)

    def f_y_recv(m, k):
        block = mats[m].at[order(k) * 2 + 1 - y]
        send(block, block, far_send.at[m, 6 + k], far_recv.at[m, 6 + k], at_y).wait_recv()

    def f_first(m):
        owns[m].wait()
        for i, q_from in enumerate((q_core, q_x, q_diag)):
            block = mats[m].at[z * 2 + y, pl.ds(pl.multiple_of(q_from * shard, 64), shard)]
            send(block, block, first_send.at[m, i], first_recv.at[m, i], at_core).wait_recv()
        f_y(m, 0).start()

    def f_pass(m, k):
        f_z_recv(m, k)
        z_start(f_z(m, k))
        f_y(m, k).start()

    def o_block(zz):
        return wo.at[zz, :, x_rows, my_half]

    def o_z(k):
        return along_z(o_block, lambda i: o_send.at[1 + i], lambda i: o_recv.at[1 + i], k)

    def o_x(k):
        block = o_block(order(k))
        return send(block, block, o_send.at[8 + k], o_recv.at[8 + k], at_x)

    def o_c(k):
        block = wo.at[order(k), :, :, my_half]
        return send(block, block, o_send.at[12 + k], o_recv.at[12 + k], at_core)

    def o_y():
        block = wo.at[z, y, x_rows, my_half]
        return send(block, block, o_send.at[1], o_recv.at[1], at_y)

    def o_first():
        o_own.wait()
        block = wo.at[z, y, core_rows, my_half]
        send(block, block, o_send.at[0], o_recv.at[0], at_core).wait_recv()
        o_y().start()

    def o_second():
        block = wo.at[z, 1 - y, x_rows, my_half]
        send(block, block, o_send.at[1], o_recv.at[1], at_y).wait_recv()
        z_start(o_z(0))
        o_x(0).start()

    def o_pass(k):
        block = o_block(order(k))
        send(block, block, o_send.at[1 + k], o_recv.at[1 + k], at_y).wait_recv()
        z_start(o_z(k))
        o_x(k).start()

    def o_share(k):
        block = wo.at[order(k), :, other_x_rows, my_half]
        send(block, block, o_send.at[8 + k], o_recv.at[8 + k], at_x).wait_recv()
        o_c(k).start()

    def o_shared(k):
        block = wo.at[order(k), :, :, other_half]
        send(block, block, o_send.at[12 + k], o_recv.at[12 + k], at_core).wait_recv()

    def z_open(m):
        z_start(f_z(m, 0))

    o_first()
    f_first(0)
    o_second()

    events = {
        0: lambda: f_first(1),
        1: lambda: (z_open(0), o_pass(1), o_share(0)),
        2: lambda: f_first(2),
        3: lambda: (o_pass(2), z_open(1)),
        4: lambda: (o_share(1), f_pass(0, 1)),
        5: lambda: (o_pass(3), o_share(2)),
        6: lambda: (f_pass(0, 2), z_open(2)),
        7: lambda: (f_pass(1, 1), f_pass(0, 3)),
    }

    lam = scale_ref[0]
    bias = bias_ref[...]
    causal = jnp.where(
        lax.broadcasted_iota(jnp.int32, (rows, rows), 1)
        <= lax.broadcasted_iota(jnp.int32, (rows, rows), 0),
        0.0,
        NEG_FILL,
    ).astype(F32)

    def head_step(h, carry):
        for copy in load(h):
            copy.wait()
        values = kv_buf[h, :, wide:]
        mixed = []
        for one in range(2):
            lanes = slice(one * half, (one + 1) * half)
            score = lax.dot_general(
                q_buf[h, :, lanes], kv_buf[h, :, lanes], (((1,), (1,)), ((), ())),
                preferred_element_type=F32,
            ) * (half ** -0.5)
            cached = bias.shape[1]
            score = jnp.concatenate(
                [score[:, :cached] + bias, score[:, cached:] + causal], axis=1
            )
            expo = jnp.exp(score - jnp.max(score, axis=1, keepdims=True))
            total = jnp.sum(expo, axis=1, keepdims=True)
            mixed.append(jnp.dot(expo.astype(BF16), values, preferred_element_type=F32) / total)
        mix = mixed[0] - lam * mixed[1]
        mix = mix * lax.rsqrt(jnp.mean(mix * mix, axis=1, keepdims=True) + 1e-05)
        mix = mix * gain_ref[...] * (1.0 - LAMBDA_BASE)
        attn[:, pl.ds(pl.multiple_of(h * wide, 128), wide)] = mix.astype(BF16)
        for i, event in events.items():
            @pl.when(h == i)
            def _(event=event):
                event()
        return carry

    lax.fori_loop(0, heads, head_step, 0)

    o_share(3)
    f_pass(1, 2)
    f_pass(1, 3)
    for k in range(4):
        o_shared(k)

    tile = 2 * half

    def project(n, carry):
        lanes = pl.ds(pl.multiple_of(n * tile, 128), tile)
        weight = wo[:, :, :, lanes].reshape(width, tile)
        value = jnp.dot(attn[...], weight, preferred_element_type=F32)
        stream[:, lanes] = (residual_ref[:, lanes].astype(F32) + value).astype(BF16)
        return carry

    lax.fori_loop(0, width // tile, project, 0)
    stream_f = stream[...].astype(F32)
    squares = jnp.mean(stream_f * stream_f, axis=1, keepdims=True)
    normed[quarter] = (stream_f * lax.rsqrt(squares + 1e-05) * norm_ref[...]).astype(BF16)

    def n_copy(q_from, i, device):
        block = normed.at[q_from]
        return send(block, block, n_send.at[i], n_recv.at[i], device)

    n_copy(quarter, 0, at_x).start()
    n_copy(quarter, 1, at_core).start()
    f_pass(2, 1)
    for m in range(2):
        for k in range(4):
            f_y_recv(m, k)

    def feed(i, carry):
        @pl.when(i == 1)
        def _():
            n_copy(q_core, 1, at_core).wait_recv()
            f_pass(2, 2)

        @pl.when(i == 2)
        def _():
            n_copy(q_x, 0, at_x).wait_recv()
            n_copy(q_x, 2, at_core).start()
            f_pass(2, 3)

        @pl.when(i == 3)
        def _():
            n_copy(q_diag, 2, at_core).wait_recv()

        slot = base_slot(i)
        tokens = normed[slot]

        def hidden_tile(n, inner_carry):
            lanes = pl.ds(pl.multiple_of(n * tile, 128), tile)
            gate = jnp.dot(tokens, wg[:, :, lanes].reshape(width, tile), preferred_element_type=F32)
            up = jnp.dot(tokens, wu[:, :, lanes].reshape(width, tile), preferred_element_type=F32)
            hidden[slot, :, lanes] = (gate / (1.0 + jnp.exp(-gate)) * up).astype(BF16)
            return inner_carry

        lax.fori_loop(0, units // tile, hidden_tile, 0)
        return carry

    def base_slot(i):
        q = (quarter + 2 * (i // 2)) % 4
        flip = i % 2
        return q + flip * (1 - 2 * (q % 2))

    lax.fori_loop(0, 4, feed, 0)

    def place(j):
        return order(j // 2) * 2 + (y + j) % 2

    def d_copy(i, p):
        if i == 0:
            return send(part.at[q_diag, p], got_core.at[0, p], d_send.at[0, p], d_recv.at[0, p], at_core)
        if i == 1:
            return send(part.at[q_core, p], got_core.at[1, p], d_send.at[1, p], d_recv.at[1, p], at_core)
        return send(to_x.at[p], got_x.at[p], d_send.at[2, p], d_recv.at[2, p], at_x)

    def d_sum(j):
        p = place(j)
        d_copy(0, p).wait_recv()
        to_x[p] = (part[q_x, p].astype(F32) + got_core[0, p].astype(F32)).astype(BF16)
        d_copy(2, p).start()

    def d_done(j):
        p = place(j)
        d_copy(1, p).wait_recv()
        d_copy(2, p).wait_recv()
        lanes = pl.ds(pl.multiple_of(p * rows, 128), rows)
        total = part[quarter, p].astype(F32) + got_core[1, p].astype(F32) + got_x[p].astype(F32)
        result_ref[:, lanes] = (stream[:, lanes].astype(F32) + total).astype(BF16)

    def down(j, carry):
        p = place(j)

        @pl.when(j % 2 == 1)
        def _():
            f_y_recv(2, j // 2)

        value = lax.dot_general(
            hidden[...].reshape(4 * rows, units), wd[p], (((1,), (1,)), ((), ())),
            preferred_element_type=F32,
        )
        value = value.astype(BF16).reshape(4, rows, value.shape[1])
        for g in range(4):
            part[g, p] = value[g]
        d_copy(0, p).start()
        d_copy(1, p).start()

        @pl.when(j >= 1)
        def _():
            d_sum(j - 1)

        @pl.when(j >= 2)
        def _():
            d_done(j - 2)

        return carry

    lax.fori_loop(0, 8, down, 0)
    d_sum(7)
    d_done(6)
    d_done(7)

    o_core.wait_send()
    o_y().wait_send()
    for group in firsts:
        for copy in group:
            copy.wait_send()
    for k in range(4):
        z_wait_send(o_z(k))
        o_x(k).wait_send()
        o_c(k).wait_send()
        for m in range(3):
            z_wait_send(f_z(m, k))
            f_y(m, k).wait_send()
    n_copy(quarter, 0, at_x).wait_send()
    n_copy(quarter, 1, at_core).wait_send()
    n_copy(q_x, 2, at_core).wait_send()

    def drain(p, carry):
        for i in range(3):
            d_copy(i, p).wait_send()
        return carry

    lax.fori_loop(0, 8, drain, 0)


def per_device_kernel(
    queries, new_kv, cache_pool, page_table, assignment, lengths, lambda_vectors, subln_gain,
    residual, out_weight, norm_gain, gate_weight, up_weight, down_weight_t,
):
    rows, heads, wide = queries.shape
    pages, page_len = cache_pool.shape[:2]
    width, units = residual.shape[1], gate_weight.shape[1] // 4
    cached = lengths[assignment[0]]
    logical = jnp.argmax(
        page_table[0][None, :] == jnp.arange(pages, dtype=jnp.int32)[:, None], axis=1
    ).astype(jnp.int32)
    position = logical[:, None] * page_len + jnp.arange(page_len, dtype=jnp.int32)[None, :]
    bias = jnp.where(position < cached, 0.0, NEG_FILL).astype(F32).reshape(1, pages * page_len)
    lam = (
        jnp.exp(jnp.sum(lambda_vectors[0] * lambda_vectors[1]))
        - jnp.exp(jnp.sum(lambda_vectors[2] * lambda_vectors[3]))
        + LAMBDA_BASE
    ).reshape(1)
    kv = jnp.concatenate([cache_pool.reshape(pages * page_len, heads, 2 * wide), new_kv], axis=0)
    kv = jnp.swapaxes(kv, 0, 1)
    keys = kv.shape[1]
    anyspace = pl.BlockSpec(memory_space=pl.ANY)
    vmem = pl.BlockSpec(memory_space=pltpu.VMEM)
    dma = pltpu.SemaphoreType.DMA
    return pl.pallas_call(
        layer_kernel,
        out_shape=jax.ShapeDtypeStruct((rows, width), BF16),
        in_specs=[pl.BlockSpec(memory_space=pltpu.SMEM)] + [vmem] * 4 + [anyspace] * 6,
        out_specs=vmem,
        scratch_shapes=[
            pltpu.VMEM((heads, rows, wide), BF16),
            pltpu.VMEM((heads, keys, 2 * wide), BF16),
            pltpu.VMEM((rows, width), BF16),
            pltpu.VMEM((4, 2, 256, width), BF16),
            pltpu.VMEM((8, 256, units), BF16),
            pltpu.VMEM((8, 256, units), BF16),
            pltpu.VMEM((8, 256, units), BF16),
            pltpu.VMEM((4, rows, width), BF16),
            pltpu.VMEM((rows, width), BF16),
            pltpu.VMEM((4, rows, units), BF16),
            pltpu.VMEM((4, 8, rows, 256), BF16),
            pltpu.VMEM((2, 8, rows, 256), BF16),
            pltpu.VMEM((8, rows, 256), BF16),
            pltpu.VMEM((8, rows, 256), BF16),
            dma((2, heads)), dma((4,)), dma((3, 3)), dma((3, 3)), dma((3, 10)), dma((3, 10)),
            dma((16,)), dma((16,)), dma((3,)), dma((3,)), dma((3, 8)), dma((3, 8)),
        ],
        compiler_params=pltpu.CompilerParams(
            collective_id=0, has_side_effects=True, vmem_limit_bytes=62 * 2**20
        ),
        name="layer",
    )(
        lam, bias, subln_gain.reshape(1, -1), norm_gain.reshape(1, -1), residual,
        jnp.swapaxes(queries, 0, 1), kv, out_weight, gate_weight, up_weight, down_weight_t,
    )


def solution(mesh):
    in_specs = (
        P("req", "mlp", None),
        P("req", "mlp", None),
        P("req", None, "mlp", None),
        P("req", None),
        P("req"),
        P(),
        P(),
        P(),
        P("req", "mlp"),
        P("req", "mlp"),
        P(),
        P("req", "mlp"),
        P("req", "mlp"),
        P("req", "mlp"),
    )
    out_specs = P("req", "mlp")
    small = mesh.shape["req"] == 32 and mesh.shape["mlp"] == 1
    return jax.shard_map(
        per_device_kernel if small else per_device, mesh=mesh, in_specs=in_specs, out_specs=out_specs, check_vma=False
    )
```

```python
import jax
import jax.numpy as jnp
from jax import lax
from jax.experimental import pallas as pl
from jax.experimental.pallas import tpu as pltpu
from jax.sharding import PartitionSpec as P

D = 2048


NEG_FILL = -1e30
LAMBDA_BASE = 0.2


def map_block(carried, query_rows, key_half, value_rows, visible, score_scale):
    running_max, running_sum, running_acc = carried
    score = (
        jnp.einsum("nhd,khd->nhk", query_rows, key_half, preferred_element_type=jnp.float32)
        * score_scale
    )
    score = jnp.where(visible[:, None, :], score, NEG_FILL)
    newest = jnp.maximum(running_max, jnp.max(score, axis=2))
    exp_terms = jnp.where(visible[:, None, :], jnp.exp(score - newest[:, :, None]), 0.0)
    shrink = jnp.exp(running_max - newest)
    running_sum = running_sum * shrink + jnp.sum(exp_terms, axis=2)
    running_acc = running_acc * shrink[:, :, None] + jnp.einsum(
        "nhk,khd->nhd",
        exp_terms.astype(jnp.bfloat16),
        value_rows,
        preferred_element_type=jnp.float32,
    )
    return (newest, running_sum, running_acc)


def both_maps(carried, query_rows, key_rows, visible, half_size):
    score_scale = half_size ** (-0.5)
    value_rows = key_rows[:, :, 2 * half_size :]
    map_one = map_block(
        carried[0],
        query_rows[:, :, :half_size],
        key_rows[:, :, :half_size],
        value_rows,
        visible,
        score_scale,
    )
    map_two = map_block(
        carried[1],
        query_rows[:, :, half_size:],
        key_rows[:, :, half_size : 2 * half_size],
        value_rows,
        visible,
        score_scale,
    )
    return (map_one, map_two)


def attend(
    queries, new_kv, cache_pool, page_table, assignment, lengths, lambda_vectors, subln_gain
):
    row_count, head_count, value_width = queries.shape
    half_size = value_width // 2
    page_len = cache_pool.shape[1]
    request = assignment[0]
    cached = jnp.sum(
        jnp.where(jnp.arange(lengths.shape[0], dtype=jnp.int32) == request, lengths, 0)
    )

    def fresh_state():
        return (
            jnp.full((row_count, head_count), NEG_FILL, jnp.float32),
            jnp.zeros((row_count, head_count), jnp.float32),
            jnp.zeros((row_count, head_count, value_width), jnp.float32),
        )

    table_row = page_table[0]

    def page_step(page_index, carried):
        physical = table_row[page_index]
        page_rows = lax.dynamic_index_in_dim(cache_pool, physical, 0, keepdims=False)
        positions = page_index * page_len + jnp.arange(page_len, dtype=jnp.int32)
        visible = jnp.broadcast_to((positions < cached)[None, :], (row_count, page_len))
        return both_maps(carried, queries, page_rows, visible, half_size)

    page_count = (cached + page_len - 1) // page_len
    carried = lax.fori_loop(jnp.int32(0), page_count, page_step, (fresh_state(), fresh_state()))
    token_pos = jnp.arange(row_count, dtype=jnp.int32)
    carried = both_maps(
        carried, queries, new_kv, token_pos[None, :] <= token_pos[:, None], half_size
    )
    lambda_now = (
        jnp.exp(jnp.sum(lambda_vectors[0] * lambda_vectors[1]))
        - jnp.exp(jnp.sum(lambda_vectors[2] * lambda_vectors[3]))
        + LAMBDA_BASE
    )
    mix_out = (
        carried[0][2] / carried[0][1][:, :, None]
        - lambda_now * carried[1][2] / carried[1][1][:, :, None]
    )
    mix_out = (
        mix_out
        * lax.rsqrt(jnp.mean(mix_out * mix_out, axis=2, keepdims=True) + 1e-05)
        * subln_gain
        * (1.0 - LAMBDA_BASE)
    )
    return mix_out.astype(jnp.bfloat16).reshape(row_count, head_count * value_width)


def per_device(
    queries,
    new_kv,
    cache_pool,
    page_table,
    assignment,
    lengths,
    lambda_vectors,
    subln_gain,
    residual,
    out_weight,
    norm_gain,
    gate_weight,
    up_weight,
    down_weight_t,
):
    attn_out = attend(
        queries, new_kv, cache_pool, page_table, assignment, lengths, lambda_vectors, subln_gain
    )
    heads_all = lax.all_gather(attn_out, "mlp", axis=1, tiled=True)
    columns = heads_all
    projected = jnp.dot(
        columns,
        lax.all_gather(out_weight, "req", axis=0, tiled=True),
        preferred_element_type=jnp.float32,
    )
    stream = (residual.astype(jnp.float32) + projected).astype(jnp.bfloat16)
    stream_f = stream.astype(jnp.float32)
    squares = lax.psum(jnp.sum(stream_f * stream_f, axis=1), "mlp")
    slice_width = stream_f.shape[1]
    local_gain = lax.dynamic_slice_in_dim(
        norm_gain, lax.axis_index("mlp") * slice_width, slice_width
    )
    normed_part = (stream_f * lax.rsqrt(squares / D + 1e-05)[:, None] * local_gain).astype(
        jnp.bfloat16
    )
    normed = lax.all_gather(normed_part, "mlp", axis=1, tiled=True)
    columns = normed
    gate_value = jnp.dot(
        columns,
        lax.all_gather(gate_weight, "req", axis=0, tiled=True),
        preferred_element_type=jnp.float32,
    )
    up_value = jnp.dot(
        columns,
        lax.all_gather(up_weight, "req", axis=0, tiled=True),
        preferred_element_type=jnp.float32,
    )
    hidden_act = (jax.nn.silu(gate_value) * up_value).astype(jnp.bfloat16)
    partial_value = lax.dot_general(
        hidden_act,
        lax.all_gather(down_weight_t, "req", axis=0, tiled=True),
        (((1,), (1,)), ((), ())),
        preferred_element_type=jnp.float32,
    )
    summed = lax.psum_scatter(
        partial_value.astype(jnp.bfloat16), "mlp", scatter_dimension=1, tiled=True
    ).astype(jnp.float32)
    return (stream_f + summed).astype(jnp.bfloat16)


BF16, F32 = jnp.bfloat16, jnp.float32
MESH = pl.DeviceIdType.MESH


def layer_kernel(
    table_ref, request_ref, lengths_ref, lambda_ref, gain_ref, norm_ref, residual_ref,
    q_hbm, kv_hbm, pool_hbm, out_hbm, gate_hbm, up_hbm, down_hbm,
    result_ref,
    q_raw, kv_raw, q_buf, kv_buf, attn, wo, wg, wu, wd, normed, stream, hidden, part, got_core, to_x, got_x,
    load_sem, own_sem, first_send, first_recv, far_send, far_recv, o_send, o_recv,
    n_send, n_recv, d_send, d_recv,
):
    heads = q_buf.shape[0]
    rows = q_buf.shape[1]
    wide = q_buf.shape[2]
    half = wide // 2
    width = stream.shape[1]
    units = wg.shape[2]
    shard = out_hbm.shape[0]
    halfw = width // 2

    me = lax.axis_index("req")
    core = me % 2
    x = (me // 2) % 2
    quarter = me % 4
    y = (me // 4) % 2
    z = me // 8
    base = me - quarter
    side = z // 2
    inner = z + side * (3 - 2 * z)
    q_core = quarter + 1 - 2 * core
    q_x = (quarter + 2) % 4
    q_diag = (q_core + 2) % 4
    at_core, at_x, at_diag = base + q_core, base + q_x, base + q_diag
    at_y = me + 4 - 8 * y
    off = me - 8 * z
    at_n = off + 8 * (1 + side)
    at_e = off + 8 * (3 * side)
    at_m = off + 8 * (2 - side)
    is_end = inner == 0
    is_mid = inner == 1

    def order(k):
        o = k + inner * (1 - 2 * k) * (1 - k // 2)
        return o + side * (3 - 2 * o)

    def send(src, dst, ssem, rsem, device):
        return pltpu.make_async_remote_copy(
            src_ref=src, dst_ref=dst, send_sem=ssem, recv_sem=rsem,
            device_id={"req": device}, device_id_type=MESH,
        )

    barrier = pltpu.get_barrier_semaphore()

    def greet(device):
        pl.semaphore_signal(barrier, inc=1, device_id={"req": device}, device_id_type=MESH)

    for device in (at_core, at_x, at_diag, at_y):
        greet(device)

    @pl.when(is_end)
    def _():
        greet(at_n)
        pl.semaphore_wait(barrier, 5)

    @pl.when(is_mid)
    def _():
        greet(at_e)
        greet(at_m)
        pl.semaphore_wait(barrier, 6)

    my_half = pl.ds(pl.multiple_of(core * halfw, 128), halfw)
    other_half = pl.ds(pl.multiple_of((1 - core) * halfw, 128), halfw)
    my_rows = pl.ds(pl.multiple_of(quarter * shard, 64), shard)
    core_rows = pl.ds(pl.multiple_of(q_core * shard, 64), shard)
    x_rows = pl.ds(pl.multiple_of(x * 2 * shard, 128), 2 * shard)
    other_x_rows = pl.ds(pl.multiple_of((1 - x) * 2 * shard, 128), 2 * shard)

    o_own = pltpu.make_async_copy(out_hbm.at[:, my_half], wo.at[z, y, my_rows, my_half], own_sem.at[0])
    o_own.start()
    o_core = send(
        out_hbm.at[:, other_half], wo.at[z, y, my_rows, other_half], o_send.at[0], o_recv.at[0], at_core
    )
    o_core.start()

    firsts = []
    owns = []
    for m, (src, dst) in enumerate(((gate_hbm, wg), (up_hbm, wu), (down_hbm, wd))):
        block = dst.at[z * 2 + y, my_rows]
        mine = pltpu.make_async_copy(
            src.at[:, pl.ds(pl.multiple_of(quarter * units, 128), units)], block, own_sem.at[1 + m]
        )
        mine.start()
        owns.append(mine)
        group = []
        for k, (q_to, device) in enumerate(((q_core, at_core), (q_x, at_x), (q_diag, at_diag))):
            copy = send(
                src.at[:, pl.ds(pl.multiple_of(q_to * units, 128), units)],
                block, first_send.at[m, k], first_recv.at[m, k], device,
            )
            copy.start()
            group.append(copy)
        firsts.append(group)

    pages, page_len = pool_hbm.shape[:2]
    chunks = pages + rows // page_len

    q_load = pltpu.make_async_copy(q_hbm, q_raw, load_sem.at[chunks])
    q_load.start()

    def chunk_load(i):
        if i < pages:
            src = pool_hbm.at[i]
        else:
            src = kv_hbm.at[pl.ds((i - pages) * page_len, page_len)]
        return pltpu.make_async_copy(src, kv_raw.at[i], load_sem.at[i])

    for i in range(chunks):
        chunk_load(i).start()

    mats = (wg, wu, wd)

    def along_z(block_at, send_sems, recv_sems, k):
        block = block_at(order(k))

        def to_end(slot):
            return send(block, block, send_sems(slot), recv_sems(slot), at_e)

        def to_mid(slot, at):
            return send(block, block, send_sems(at), recv_sems(slot), at_m)

        if k == 0:
            return (
                [send(block, block, send_sems(1), recv_sems(1), at_n)],
                [to_end(1), to_mid(2, 4)],
            )
        if k == 1:
            return [], [to_mid(3, 5)]
        return [], [to_end(k)]

    def z_start(copies):
        for_end, for_mid = copies
        if for_end:
            @pl.when(is_end)
            def _():
                for copy in for_end:
                    copy.start()

        @pl.when(is_mid)
        def _():
            for copy in for_mid:
                copy.start()

    def z_wait_send(copies):
        for_end, for_mid = copies
        if for_end:
            @pl.when(is_end)
            def _():
                for copy in for_end:
                    copy.wait_send()

        @pl.when(is_mid)
        def _():
            for copy in for_mid:
                copy.wait_send()

    def f_block(m):
        return lambda zz: mats[m].at[zz * 2 + y]

    def f_z(m, k):
        return along_z(
            f_block(m), lambda i: far_send.at[m, i], lambda i: far_recv.at[m, i], k
        )

    def f_z_recv(m, k):
        block = f_block(m)(order(k))
        send(block, block, far_send.at[m, k], far_recv.at[m, k], at_y).wait_recv()

    def f_y(m, k):
        block = f_block(m)(order(k))
        return send(block, block, far_send.at[m, 6 + k], far_recv.at[m, 6 + k], at_y)

    def f_y_recv(m, k):
        block = mats[m].at[order(k) * 2 + 1 - y]
        send(block, block, far_send.at[m, 6 + k], far_recv.at[m, 6 + k], at_y).wait_recv()

    def f_first(m):
        owns[m].wait()
        for i, q_from in enumerate((q_core, q_x, q_diag)):
            block = mats[m].at[z * 2 + y, pl.ds(pl.multiple_of(q_from * shard, 64), shard)]
            send(block, block, first_send.at[m, i], first_recv.at[m, i], at_core).wait_recv()
        f_y(m, 0).start()

    def f_pass(m, k):
        f_z_recv(m, k)
        z_start(f_z(m, k))
        f_y(m, k).start()

    def o_block(zz):
        return wo.at[zz, :, x_rows, my_half]

    def o_z(k):
        return along_z(o_block, lambda i: o_send.at[1 + i], lambda i: o_recv.at[1 + i], k)

    def o_x(k):
        block = o_block(order(k))
        return send(block, block, o_send.at[8 + k], o_recv.at[8 + k], at_x)

    def o_c(k):
        block = wo.at[order(k), :, :, my_half]
        return send(block, block, o_send.at[12 + k], o_recv.at[12 + k], at_core)

    def o_y():
        block = wo.at[z, y, x_rows, my_half]
        return send(block, block, o_send.at[1], o_recv.at[1], at_y)

    def o_first():
        o_own.wait()
        block = wo.at[z, y, core_rows, my_half]
        send(block, block, o_send.at[0], o_recv.at[0], at_core).wait_recv()
        o_y().start()

    def o_second():
        block = wo.at[z, 1 - y, x_rows, my_half]
        send(block, block, o_send.at[1], o_recv.at[1], at_y).wait_recv()
        z_start(o_z(0))
        o_x(0).start()

    def o_pass(k):
        block = o_block(order(k))
        send(block, block, o_send.at[1 + k], o_recv.at[1 + k], at_y).wait_recv()
        z_start(o_z(k))
        o_x(k).start()

    def o_share(k):
        block = wo.at[order(k), :, other_x_rows, my_half]
        send(block, block, o_send.at[8 + k], o_recv.at[8 + k], at_x).wait_recv()
        o_c(k).start()

    def o_shared(k):
        block = wo.at[order(k), :, :, other_half]
        send(block, block, o_send.at[12 + k], o_recv.at[12 + k], at_core).wait_recv()

    def z_open(m):
        z_start(f_z(m, 0))

    def split(at_mid, at_end):
        @pl.when(is_mid)
        def _():
            at_mid()

        @pl.when(is_end)
        def _():
            at_end()

    def run_events(step, at_mid, at_end):
        for place_at, events in ((is_mid, at_mid), (is_end, at_end)):
            for i, event in events.items():
                @pl.when(jnp.logical_and(place_at, step == i))
                def _(event=event):
                    event()

    o_first()

    q_load.wait()
    for i in range(rows // page_len):
        span = pl.ds(i * page_len, page_len)
        q_buf[:, span, :] = jnp.swapaxes(q_raw[span], 0, 1)

    chunk_events = {1: o_second, 3: lambda: f_first(0), 5: lambda: f_first(1), 7: lambda: f_first(2)}

    def turn(i, carry):
        pltpu.make_async_copy(pool_hbm.at[0], kv_raw.at[i], load_sem.at[i]).wait()
        span = pl.ds(pl.multiple_of(i * page_len, page_len), page_len)
        kv_buf[:, span, :] = jnp.swapaxes(kv_raw[i], 0, 1)
        run_events(i, chunk_events, chunk_events)
        return carry

    lax.fori_loop(0, chunks, turn, 0)

    mid_events = {
        3: lambda: (o_pass(2), o_pass(1), o_share(0), z_open(0)),
        6: lambda: (o_share(1), o_pass(3)),
        7: lambda: (f_pass(0, 1), z_open(1), o_share(2)),
    }
    end_events = {
        2: lambda: z_open(0),
        3: lambda: (o_pass(1), o_share(0)),
        4: lambda: z_open(1),
        6: lambda: (o_share(1), z_open(2)),
        7: lambda: o_pass(2),
    }

    vectors = lambda_ref[...]
    lam = (
        jnp.exp(jnp.sum(vectors[0:1] * vectors[1:2], axis=1, keepdims=True))
        - jnp.exp(jnp.sum(vectors[2:3] * vectors[3:4], axis=1, keepdims=True))
        + LAMBDA_BASE
    )
    length = lengths_ref[request_ref[0]]
    within = lax.broadcasted_iota(jnp.int32, (1, page_len), 1)
    pieces = []
    for page in range(pages):
        logical = jnp.int32(0)
        for j in range(pages):
            logical = logical + jnp.where(table_ref[0, j] == page, j, 0)
        pieces.append(jnp.where(within + logical * page_len < length, 0.0, NEG_FILL))
    bias = jnp.concatenate(pieces, axis=1).astype(F32)
    causal = jnp.where(
        lax.broadcasted_iota(jnp.int32, (rows, rows), 1)
        <= lax.broadcasted_iota(jnp.int32, (rows, rows), 0),
        0.0,
        NEG_FILL,
    ).astype(F32)

    def head_step(h, carry):
        values = kv_buf[h, :, wide:]
        mixed = []
        for one in range(2):
            lanes = slice(one * half, (one + 1) * half)
            score = lax.dot_general(
                q_buf[h, :, lanes], kv_buf[h, :, lanes], (((1,), (1,)), ((), ())),
                preferred_element_type=F32,
            ) * (half ** -0.5)
            cached = bias.shape[1]
            score = jnp.concatenate(
                [score[:, :cached] + bias, score[:, cached:] + causal], axis=1
            )
            expo = jnp.exp(score - jnp.max(score, axis=1, keepdims=True))
            total = jnp.sum(expo, axis=1, keepdims=True)
            mixed.append(jnp.dot(expo.astype(BF16), values, preferred_element_type=F32) / total)
        mix = mixed[0] - lam * mixed[1]
        mix = mix * lax.rsqrt(jnp.mean(mix * mix, axis=1, keepdims=True) + 1e-05)
        mix = mix * gain_ref[...] * (1.0 - LAMBDA_BASE)
        attn[:, pl.ds(pl.multiple_of(h * wide, 128), wide)] = mix.astype(BF16)
        run_events(h, mid_events, end_events)
        return carry

    lax.fori_loop(0, heads, head_step, 0)

    split(
        lambda: (f_pass(0, 2), o_share(3), f_pass(0, 3)),
        lambda: (o_share(2), o_pass(3), f_pass(0, 1), o_share(3)),
    )
    for k in range(4):
        o_shared(k)

    tile = 2 * half

    def project(n, carry):
        lanes = pl.ds(pl.multiple_of(n * tile, 128), tile)
        weight = wo[:, :, :, lanes].reshape(width, tile)
        value = jnp.dot(attn[...], weight, preferred_element_type=F32)
        stream[:, lanes] = (residual_ref[:, lanes].astype(F32) + value).astype(BF16)
        return carry

    lax.fori_loop(0, width // tile, project, 0)
    stream_f = stream[...].astype(F32)
    squares = jnp.mean(stream_f * stream_f, axis=1, keepdims=True)
    normed[quarter] = (stream_f * lax.rsqrt(squares + 1e-05) * norm_ref[...]).astype(BF16)

    def n_copy(q_from, i, device):
        block = normed.at[q_from]
        return send(block, block, n_send.at[i], n_recv.at[i], device)

    n_copy(quarter, 0, at_x).start()
    n_copy(quarter, 1, at_core).start()
    def relay():
        n_copy(q_x, 0, at_x).wait_recv()
        n_copy(q_x, 2, at_core).start()

    split(
        lambda: (
            f_pass(1, 1), f_pass(1, 2), f_pass(1, 3), z_open(2), relay(),
            f_pass(2, 1), f_pass(2, 2), f_pass(2, 3),
        ),
        lambda: (
            f_pass(0, 2), f_pass(0, 3), f_pass(1, 1), relay(), f_pass(1, 2), f_pass(1, 3),
        ),
    )
    for m in range(2):
        for k in range(4):
            f_y_recv(m, k)

    feed_events = {1: lambda: f_pass(2, 1), 3: lambda: f_pass(2, 2)}

    def feed(i, carry):
        run_events(i, {}, feed_events)

        @pl.when(i == 1)
        def _():
            n_copy(q_core, 1, at_core).wait_recv()

        @pl.when(i == 3)
        def _():
            n_copy(q_diag, 2, at_core).wait_recv()

        slot = base_slot(i)
        tokens = normed[slot]

        def hidden_tile(n, inner_carry):
            lanes = pl.ds(pl.multiple_of(n * tile, 128), tile)
            gate = jnp.dot(tokens, wg[:, :, lanes].reshape(width, tile), preferred_element_type=F32)
            up = jnp.dot(tokens, wu[:, :, lanes].reshape(width, tile), preferred_element_type=F32)
            hidden[slot, :, lanes] = (gate / (1.0 + jnp.exp(-gate)) * up).astype(BF16)
            return inner_carry

        lax.fori_loop(0, units // tile, hidden_tile, 0)
        return carry

    def base_slot(i):
        q = (quarter + 2 * (i // 2)) % 4
        flip = i % 2
        return q + flip * (1 - 2 * (q % 2))

    lax.fori_loop(0, 4, feed, 0)

    def place(j):
        return order(j // 2) * 2 + (y + j) % 2

    def d_copy(i, p):
        if i == 0:
            return send(part.at[q_diag, p], got_core.at[0, p], d_send.at[0, p], d_recv.at[0, p], at_core)
        if i == 1:
            return send(part.at[q_core, p], got_core.at[1, p], d_send.at[1, p], d_recv.at[1, p], at_core)
        return send(to_x.at[p], got_x.at[p], d_send.at[2, p], d_recv.at[2, p], at_x)

    def d_sum(j):
        p = place(j)
        d_copy(0, p).wait_recv()
        to_x[p] = (part[q_x, p].astype(F32) + got_core[0, p].astype(F32)).astype(BF16)
        d_copy(2, p).start()

    def d_done(j):
        p = place(j)
        d_copy(1, p).wait_recv()
        d_copy(2, p).wait_recv()
        lanes = pl.ds(pl.multiple_of(p * rows, 128), rows)
        total = part[quarter, p].astype(F32) + got_core[1, p].astype(F32) + got_x[p].astype(F32)
        result_ref[:, lanes] = (stream[:, lanes].astype(F32) + total).astype(BF16)

    def down(j, carry):
        p = place(j)

        @pl.when(j % 2 == 1)
        def _():
            f_y_recv(2, j // 2)

        value = lax.dot_general(
            hidden[...].reshape(4 * rows, units), wd[p], (((1,), (1,)), ((), ())),
            preferred_element_type=F32,
        )
        value = value.astype(BF16).reshape(4, rows, value.shape[1])
        for g in range(4):
            part[g, p] = value[g]
        d_copy(0, p).start()
        d_copy(1, p).start()

        run_events(j, {}, {5: lambda: f_pass(2, 3)})

        @pl.when(j >= 1)
        def _():
            d_sum(j - 1)

        @pl.when(j >= 2)
        def _():
            d_done(j - 2)

        return carry

    lax.fori_loop(0, 8, down, 0)
    d_sum(7)
    d_done(6)
    d_done(7)

    o_core.wait_send()
    o_y().wait_send()
    for group in firsts:
        for copy in group:
            copy.wait_send()
    for k in range(4):
        z_wait_send(o_z(k))
        o_x(k).wait_send()
        o_c(k).wait_send()
        for m in range(3):
            z_wait_send(f_z(m, k))
            f_y(m, k).wait_send()
    n_copy(quarter, 0, at_x).wait_send()
    n_copy(quarter, 1, at_core).wait_send()
    n_copy(q_x, 2, at_core).wait_send()

    def drain(p, carry):
        for i in range(3):
            d_copy(i, p).wait_send()
        return carry

    lax.fori_loop(0, 8, drain, 0)


def per_device_kernel(
    queries, new_kv, cache_pool, page_table, assignment, lengths, lambda_vectors, subln_gain,
    residual, out_weight, norm_gain, gate_weight, up_weight, down_weight_t,
):
    rows, heads, wide = queries.shape
    pages, page_len = cache_pool.shape[:2]
    width, units = residual.shape[1], gate_weight.shape[1] // 4
    keys = pages * page_len + rows
    anyspace = pl.BlockSpec(memory_space=pl.ANY)
    vmem = pl.BlockSpec(memory_space=pltpu.VMEM)
    dma = pltpu.SemaphoreType.DMA
    return pl.pallas_call(
        layer_kernel,
        out_shape=jax.ShapeDtypeStruct((rows, width), BF16),
        in_specs=[pl.BlockSpec(memory_space=pltpu.SMEM)] * 3 + [vmem] * 4 + [anyspace] * 7,
        out_specs=vmem,
        scratch_shapes=[
            pltpu.VMEM((rows, heads, wide), BF16),
            pltpu.VMEM((keys // page_len, page_len, heads, 2 * wide), BF16),
            pltpu.VMEM((heads, rows, wide), BF16),
            pltpu.VMEM((heads, keys, 2 * wide), BF16),
            pltpu.VMEM((rows, width), BF16),
            pltpu.VMEM((4, 2, 256, width), BF16),
            pltpu.VMEM((8, 256, units), BF16),
            pltpu.VMEM((8, 256, units), BF16),
            pltpu.VMEM((8, 256, units), BF16),
            pltpu.VMEM((4, rows, width), BF16),
            pltpu.VMEM((rows, width), BF16),
            pltpu.VMEM((4, rows, units), BF16),
            pltpu.VMEM((4, 8, rows, 256), BF16),
            pltpu.VMEM((2, 8, rows, 256), BF16),
            pltpu.VMEM((8, rows, 256), BF16),
            pltpu.VMEM((8, rows, 256), BF16),
            dma((keys // page_len + 1,)), dma((4,)), dma((3, 3)), dma((3, 3)), dma((3, 10)), dma((3, 10)),
            dma((16,)), dma((16,)), dma((3,)), dma((3,)), dma((3, 8)), dma((3, 8)),
        ],
        compiler_params=pltpu.CompilerParams(
            collective_id=0, has_side_effects=True, vmem_limit_bytes=62 * 2**20
        ),
        name="layer",
    )(
        page_table, assignment, lengths, lambda_vectors, subln_gain.reshape(1, -1),
        norm_gain.reshape(1, -1), residual, queries, new_kv, cache_pool,
        out_weight, gate_weight, up_weight, down_weight_t,
    )


def solution(mesh):
    in_specs = (
        P("req", "mlp", None),
        P("req", "mlp", None),
        P("req", None, "mlp", None),
        P("req", None),
        P("req"),
        P(),
        P(),
        P(),
        P("req", "mlp"),
        P("req", "mlp"),
        P(),
        P("req", "mlp"),
        P("req", "mlp"),
        P("req", "mlp"),
    )
    out_specs = P("req", "mlp")
    small = mesh.shape["req"] == 32 and mesh.shape["mlp"] == 1
    return jax.shard_map(
        per_device_kernel if small else per_device, mesh=mesh, in_specs=in_specs, out_specs=out_specs, check_vma=False
    )
```

```python
import jax
import jax.numpy as jnp
from jax import lax
from jax.experimental import pallas as pl
from jax.experimental.pallas import tpu as pltpu
from jax.sharding import PartitionSpec as P

D = 2048


NEG_FILL = -1e30
LAMBDA_BASE = 0.2


def map_block(carried, query_rows, key_half, value_rows, visible, score_scale):
    running_max, running_sum, running_acc = carried
    score = (
        jnp.einsum("nhd,khd->nhk", query_rows, key_half, preferred_element_type=jnp.float32)
        * score_scale
    )
    score = jnp.where(visible[:, None, :], score, NEG_FILL)
    newest = jnp.maximum(running_max, jnp.max(score, axis=2))
    exp_terms = jnp.where(visible[:, None, :], jnp.exp(score - newest[:, :, None]), 0.0)
    shrink = jnp.exp(running_max - newest)
    running_sum = running_sum * shrink + jnp.sum(exp_terms, axis=2)
    running_acc = running_acc * shrink[:, :, None] + jnp.einsum(
        "nhk,khd->nhd",
        exp_terms.astype(jnp.bfloat16),
        value_rows,
        preferred_element_type=jnp.float32,
    )
    return (newest, running_sum, running_acc)


def both_maps(carried, query_rows, key_rows, visible, half_size):
    score_scale = half_size ** (-0.5)
    value_rows = key_rows[:, :, 2 * half_size :]
    map_one = map_block(
        carried[0],
        query_rows[:, :, :half_size],
        key_rows[:, :, :half_size],
        value_rows,
        visible,
        score_scale,
    )
    map_two = map_block(
        carried[1],
        query_rows[:, :, half_size:],
        key_rows[:, :, half_size : 2 * half_size],
        value_rows,
        visible,
        score_scale,
    )
    return (map_one, map_two)


def attend(
    queries, new_kv, cache_pool, page_table, assignment, lengths, lambda_vectors, subln_gain
):
    row_count, head_count, value_width = queries.shape
    half_size = value_width // 2
    page_len = cache_pool.shape[1]
    request = assignment[0]
    cached = jnp.sum(
        jnp.where(jnp.arange(lengths.shape[0], dtype=jnp.int32) == request, lengths, 0)
    )

    def fresh_state():
        return (
            jnp.full((row_count, head_count), NEG_FILL, jnp.float32),
            jnp.zeros((row_count, head_count), jnp.float32),
            jnp.zeros((row_count, head_count, value_width), jnp.float32),
        )

    table_row = page_table[0]

    def page_step(page_index, carried):
        physical = table_row[page_index]
        page_rows = lax.dynamic_index_in_dim(cache_pool, physical, 0, keepdims=False)
        positions = page_index * page_len + jnp.arange(page_len, dtype=jnp.int32)
        visible = jnp.broadcast_to((positions < cached)[None, :], (row_count, page_len))
        return both_maps(carried, queries, page_rows, visible, half_size)

    page_count = (cached + page_len - 1) // page_len
    carried = lax.fori_loop(jnp.int32(0), page_count, page_step, (fresh_state(), fresh_state()))
    token_pos = jnp.arange(row_count, dtype=jnp.int32)
    carried = both_maps(
        carried, queries, new_kv, token_pos[None, :] <= token_pos[:, None], half_size
    )
    lambda_now = (
        jnp.exp(jnp.sum(lambda_vectors[0] * lambda_vectors[1]))
        - jnp.exp(jnp.sum(lambda_vectors[2] * lambda_vectors[3]))
        + LAMBDA_BASE
    )
    mix_out = (
        carried[0][2] / carried[0][1][:, :, None]
        - lambda_now * carried[1][2] / carried[1][1][:, :, None]
    )
    mix_out = (
        mix_out
        * lax.rsqrt(jnp.mean(mix_out * mix_out, axis=2, keepdims=True) + 1e-05)
        * subln_gain
        * (1.0 - LAMBDA_BASE)
    )
    return mix_out.astype(jnp.bfloat16).reshape(row_count, head_count * value_width)


def per_device(
    queries,
    new_kv,
    cache_pool,
    page_table,
    assignment,
    lengths,
    lambda_vectors,
    subln_gain,
    residual,
    out_weight,
    norm_gain,
    gate_weight,
    up_weight,
    down_weight_t,
):
    attn_out = attend(
        queries, new_kv, cache_pool, page_table, assignment, lengths, lambda_vectors, subln_gain
    )
    heads_all = lax.all_gather(attn_out, "mlp", axis=1, tiled=True)
    columns = heads_all
    projected = jnp.dot(
        columns,
        lax.all_gather(out_weight, "req", axis=0, tiled=True),
        preferred_element_type=jnp.float32,
    )
    stream = (residual.astype(jnp.float32) + projected).astype(jnp.bfloat16)
    stream_f = stream.astype(jnp.float32)
    squares = lax.psum(jnp.sum(stream_f * stream_f, axis=1), "mlp")
    slice_width = stream_f.shape[1]
    local_gain = lax.dynamic_slice_in_dim(
        norm_gain, lax.axis_index("mlp") * slice_width, slice_width
    )
    normed_part = (stream_f * lax.rsqrt(squares / D + 1e-05)[:, None] * local_gain).astype(
        jnp.bfloat16
    )
    normed = lax.all_gather(normed_part, "mlp", axis=1, tiled=True)
    columns = normed
    gate_value = jnp.dot(
        columns,
        lax.all_gather(gate_weight, "req", axis=0, tiled=True),
        preferred_element_type=jnp.float32,
    )
    up_value = jnp.dot(
        columns,
        lax.all_gather(up_weight, "req", axis=0, tiled=True),
        preferred_element_type=jnp.float32,
    )
    hidden_act = (jax.nn.silu(gate_value) * up_value).astype(jnp.bfloat16)
    partial_value = lax.dot_general(
        hidden_act,
        lax.all_gather(down_weight_t, "req", axis=0, tiled=True),
        (((1,), (1,)), ((), ())),
        preferred_element_type=jnp.float32,
    )
    summed = lax.psum_scatter(
        partial_value.astype(jnp.bfloat16), "mlp", scatter_dimension=1, tiled=True
    ).astype(jnp.float32)
    return (stream_f + summed).astype(jnp.bfloat16)


BF16, F32 = jnp.bfloat16, jnp.float32
MESH = pl.DeviceIdType.MESH


def layer_kernel(
    table_ref, request_ref, lengths_ref, lambda_ref, gain_ref, norm_ref, residual_ref,
    q_hbm, kv_hbm, pool_hbm, out_hbm, gate_hbm, up_hbm, down_hbm,
    result_ref,
    q_raw, kv_raw, q_buf, kv_buf, attn, wo, wg, wu, wd, normed, stream, hidden, part, got_core, to_x, got_x,
    load_sem, own_sem, first_send, first_recv, far_send, far_recv, oz_send, oz_recv, o_send, o_recv,
    n_send, n_recv, d_send, d_recv,
):
    heads = q_buf.shape[0]
    rows = q_buf.shape[1]
    wide = q_buf.shape[2]
    half = wide // 2
    width = stream.shape[1]
    units = wg.shape[2]
    shard = out_hbm.shape[0]
    halfw = width // 2

    me = lax.axis_index("req")
    core = me % 2
    x = (me // 2) % 2
    quarter = me % 4
    y = (me // 4) % 2
    z = me // 8
    base = me - quarter
    side = z // 2
    inner = z + side * (3 - 2 * z)
    q_core = quarter + 1 - 2 * core
    q_x = (quarter + 2) % 4
    q_diag = (q_core + 2) % 4
    at_core, at_x, at_diag = base + q_core, base + q_x, base + q_diag
    at_y = me + 4 - 8 * y
    off = me - 8 * z
    at_n = off + 8 * (1 + side)
    at_e = off + 8 * (3 * side)
    at_m = off + 8 * (2 - side)
    is_end = inner == 0
    is_mid = inner == 1

    def order(k):
        o = k + inner * (1 - 2 * k) * (1 - k // 2)
        return o + side * (3 - 2 * o)

    def send(src, dst, ssem, rsem, device):
        return pltpu.make_async_remote_copy(
            src_ref=src, dst_ref=dst, send_sem=ssem, recv_sem=rsem,
            device_id={"req": device}, device_id_type=MESH,
        )

    barrier = pltpu.get_barrier_semaphore()

    def greet(device):
        pl.semaphore_signal(barrier, inc=1, device_id={"req": device}, device_id_type=MESH)

    for device in (at_core, at_x, at_diag, at_y):
        greet(device)

    @pl.when(is_end)
    def _():
        greet(at_n)
        pl.semaphore_wait(barrier, 5)

    @pl.when(is_mid)
    def _():
        greet(at_e)
        greet(at_m)
        pl.semaphore_wait(barrier, 6)

    my_half = pl.ds(pl.multiple_of(core * halfw, 128), halfw)
    other_half = pl.ds(pl.multiple_of((1 - core) * halfw, 128), halfw)
    my_rows = pl.ds(pl.multiple_of(quarter * shard, 64), shard)
    core_rows = pl.ds(pl.multiple_of(q_core * shard, 64), shard)
    x_rows = pl.ds(pl.multiple_of(x * 2 * shard, 128), 2 * shard)
    other_x_rows = pl.ds(pl.multiple_of((1 - x) * 2 * shard, 128), 2 * shard)

    o_own = pltpu.make_async_copy(out_hbm.at[:, my_half], wo.at[z, y, my_rows, my_half], own_sem.at[0])
    o_own.start()
    o_core = send(
        out_hbm.at[:, other_half], wo.at[z, y, my_rows, other_half], o_send.at[0], o_recv.at[0], at_core
    )
    o_core.start()

    firsts = []
    owns = []
    for m, (src, dst) in enumerate(((gate_hbm, wg), (up_hbm, wu), (down_hbm, wd))):
        block = dst.at[z * 2 + y, my_rows]
        mine = pltpu.make_async_copy(
            src.at[:, pl.ds(pl.multiple_of(quarter * units, 128), units)], block, own_sem.at[1 + m]
        )
        mine.start()
        owns.append(mine)
        group = []
        for k, (q_to, device) in enumerate(((q_core, at_core), (q_x, at_x), (q_diag, at_diag))):
            copy = send(
                src.at[:, pl.ds(pl.multiple_of(q_to * units, 128), units)],
                block, first_send.at[m, k], first_recv.at[m, k], device,
            )
            copy.start()
            group.append(copy)
        firsts.append(group)

    pages, page_len = pool_hbm.shape[:2]
    chunks = pages + rows // page_len

    q_load = pltpu.make_async_copy(q_hbm, q_raw, load_sem.at[chunks])
    q_load.start()

    def chunk_load(i):
        if i < pages:
            src = pool_hbm.at[i]
        else:
            src = kv_hbm.at[pl.ds((i - pages) * page_len, page_len)]
        return pltpu.make_async_copy(src, kv_raw.at[i], load_sem.at[i])

    for i in range(chunks):
        chunk_load(i).start()

    mats = (wg, wu, wd)

    def along_z(block_at, send_sems, recv_sems, k):
        block = block_at(order(k))

        def to_end(slot):
            return send(block, block, send_sems(slot), recv_sems(slot), at_e)

        def to_mid(slot, at):
            return send(block, block, send_sems(at), recv_sems(slot), at_m)

        if k == 0:
            return (
                [send(block, block, send_sems(1), recv_sems(1), at_n)],
                [to_end(1), to_mid(2, 4)],
            )
        if k == 1:
            return [], [to_mid(3, 5)]
        return [], [to_end(k)]

    def z_start(copies):
        for_end, for_mid = copies
        if for_end:
            @pl.when(is_end)
            def _():
                for copy in for_end:
                    copy.start()

        @pl.when(is_mid)
        def _():
            for copy in for_mid:
                copy.start()

    def z_wait_send(copies):
        for_end, for_mid = copies
        if for_end:
            @pl.when(is_end)
            def _():
                for copy in for_end:
                    copy.wait_send()

        @pl.when(is_mid)
        def _():
            for copy in for_mid:
                copy.wait_send()

    def f_block(m, part):
        span = pl.ds(part * (mats[m].shape[1] // 2), mats[m].shape[1] // 2)
        return lambda zz: mats[m].at[zz * 2 + y, span]

    def f_z(m, k, part):
        return along_z(
            f_block(m, part),
            lambda i: far_send.at[m, part, i],
            lambda i: far_recv.at[m, part, i],
            k,
        )

    def f_z_recv(m, k, part):
        block = f_block(m, part)(order(k))
        send(block, block, far_send.at[m, part, k], far_recv.at[m, part, k], at_y).wait_recv()

    def f_y(m, k, part):
        block = f_block(m, part)(order(k))
        return send(block, block, far_send.at[m, part, 6 + k], far_recv.at[m, part, 6 + k], at_y)

    def f_y_recv(m, k):
        for part in range(2):
            half_rows = mats[m].shape[1] // 2
            block = mats[m].at[order(k) * 2 + 1 - y, pl.ds(part * half_rows, half_rows)]
            send(
                block, block, far_send.at[m, part, 6 + k], far_recv.at[m, part, 6 + k], at_y
            ).wait_recv()

    def f_first(m):
        owns[m].wait()
        for i, q_from in enumerate((q_core, q_x, q_diag)):
            block = mats[m].at[z * 2 + y, pl.ds(pl.multiple_of(q_from * shard, 64), shard)]
            send(block, block, first_send.at[m, i], first_recv.at[m, i], at_core).wait_recv()
        for part in range(2):
            f_y(m, 0, part).start()

    def f_pass(m, k):
        for part in range(2):
            f_z_recv(m, k, part)
            z_start(f_z(m, k, part))
            f_y(m, k, part).start()

    def o_block(s):
        return lambda zz: wo.at[zz, (y + s) % 2, x_rows, my_half]

    def o_z(k, s):
        return along_z(o_block(s), lambda i: oz_send.at[s, i], lambda i: oz_recv.at[s, i], k)

    def o_x(k):
        block = wo.at[order(k), :, x_rows, my_half]
        return send(block, block, o_send.at[8 + k], o_recv.at[8 + k], at_x)

    def o_c(k):
        block = wo.at[order(k), :, :, my_half]
        return send(block, block, o_send.at[12 + k], o_recv.at[12 + k], at_core)

    def o_y():
        block = wo.at[z, y, x_rows, my_half]
        return send(block, block, o_send.at[1], o_recv.at[1], at_y)

    def o_first():
        o_own.wait()
        block = wo.at[z, y, core_rows, my_half]
        send(block, block, o_send.at[0], o_recv.at[0], at_core).wait_recv()
        z_start(o_z(0, 0))
        o_y().start()

    def o_second():
        block = wo.at[z, 1 - y, x_rows, my_half]
        send(block, block, o_send.at[1], o_recv.at[1], at_y).wait_recv()
        z_start(o_z(0, 1))
        o_x(0).start()

    def o_pass(k):
        for s in range(2):
            block = o_block(s)(order(k))
            send(block, block, oz_send.at[s, k], oz_recv.at[s, k], at_y).wait_recv()
            z_start(o_z(k, s))
        o_x(k).start()

    def o_share(k):
        block = wo.at[order(k), :, other_x_rows, my_half]
        send(block, block, o_send.at[8 + k], o_recv.at[8 + k], at_x).wait_recv()
        o_c(k).start()

    def o_shared(k):
        block = wo.at[order(k), :, :, other_half]
        send(block, block, o_send.at[12 + k], o_recv.at[12 + k], at_core).wait_recv()

    def z_open(m):
        for part in range(2):
            z_start(f_z(m, 0, part))

    def split(at_mid, at_end):
        @pl.when(is_mid)
        def _():
            at_mid()

        @pl.when(is_end)
        def _():
            at_end()

    def run_events(step, at_mid, at_end):
        for place_at, events in ((is_mid, at_mid), (is_end, at_end)):
            for i, event in events.items():
                @pl.when(jnp.logical_and(place_at, step == i))
                def _(event=event):
                    event()

    o_first()

    q_load.wait()
    for i in range(rows // page_len):
        span = pl.ds(i * page_len, page_len)
        q_buf[:, span, :] = jnp.swapaxes(q_raw[span], 0, 1)

    chunk_events = {1: o_second, 3: lambda: f_first(0), 5: lambda: f_first(1), 7: lambda: f_first(2)}

    def turn(i, carry):
        pltpu.make_async_copy(pool_hbm.at[0], kv_raw.at[i], load_sem.at[i]).wait()
        span = pl.ds(pl.multiple_of(i * page_len, page_len), page_len)
        kv_buf[:, span, :] = jnp.swapaxes(kv_raw[i], 0, 1)
        run_events(i, chunk_events, chunk_events)
        return carry

    lax.fori_loop(0, chunks, turn, 0)

    mid_events = {
        2: lambda: z_open(0),
        3: lambda: (o_pass(2), o_pass(1), o_share(0)),
        5: lambda: (o_share(1), z_open(1)),
        6: lambda: o_pass(3),
        7: lambda: (f_pass(0, 1), o_share(2)),
    }
    end_events = {
        2: lambda: z_open(0),
        3: lambda: (o_pass(1), o_share(0)),
        4: lambda: z_open(1),
        6: lambda: (o_share(1), z_open(2)),
        7: lambda: o_pass(2),
    }

    vectors = lambda_ref[...]
    lam = (
        jnp.exp(jnp.sum(vectors[0:1] * vectors[1:2], axis=1, keepdims=True))
        - jnp.exp(jnp.sum(vectors[2:3] * vectors[3:4], axis=1, keepdims=True))
        + LAMBDA_BASE
    )
    length = lengths_ref[request_ref[0]]
    within = lax.broadcasted_iota(jnp.int32, (1, page_len), 1)
    pieces = []
    for page in range(pages):
        logical = jnp.int32(0)
        for j in range(pages):
            logical = logical + jnp.where(table_ref[0, j] == page, j, 0)
        pieces.append(jnp.where(within + logical * page_len < length, 0.0, NEG_FILL))
    bias = jnp.concatenate(pieces, axis=1).astype(F32)
    causal = jnp.where(
        lax.broadcasted_iota(jnp.int32, (rows, rows), 1)
        <= lax.broadcasted_iota(jnp.int32, (rows, rows), 0),
        0.0,
        NEG_FILL,
    ).astype(F32)

    def head_step(h, carry):
        values = kv_buf[h, :, wide:]
        mixed = []
        for one in range(2):
            lanes = slice(one * half, (one + 1) * half)
            score = lax.dot_general(
                q_buf[h, :, lanes], kv_buf[h, :, lanes], (((1,), (1,)), ((), ())),
                preferred_element_type=F32,
            ) * (half ** -0.5)
            cached = bias.shape[1]
            score = jnp.concatenate(
                [score[:, :cached] + bias, score[:, cached:] + causal], axis=1
            )
            expo = jnp.exp(score - jnp.max(score, axis=1, keepdims=True))
            total = jnp.sum(expo, axis=1, keepdims=True)
            mixed.append(jnp.dot(expo.astype(BF16), values, preferred_element_type=F32) / total)
        mix = mixed[0] - lam * mixed[1]
        mix = mix * lax.rsqrt(jnp.mean(mix * mix, axis=1, keepdims=True) + 1e-05)
        mix = mix * gain_ref[...] * (1.0 - LAMBDA_BASE)
        attn[:, pl.ds(pl.multiple_of(h * wide, 128), wide)] = mix.astype(BF16)
        run_events(h, mid_events, end_events)
        return carry

    lax.fori_loop(0, heads, head_step, 0)

    split(
        lambda: (f_pass(0, 2), o_share(3), f_pass(0, 3)),
        lambda: (o_share(2), o_pass(3), f_pass(0, 1), o_share(3)),
    )
    for k in range(4):
        o_shared(k)

    tile = 2 * half

    def project(n, carry):
        lanes = pl.ds(pl.multiple_of(n * tile, 128), tile)
        weight = wo[:, :, :, lanes].reshape(width, tile)
        value = jnp.dot(attn[...], weight, preferred_element_type=F32)
        stream[:, lanes] = (residual_ref[:, lanes].astype(F32) + value).astype(BF16)
        return carry

    lax.fori_loop(0, width // tile, project, 0)
    stream_f = stream[...].astype(F32)
    squares = jnp.mean(stream_f * stream_f, axis=1, keepdims=True)
    normed[quarter] = (stream_f * lax.rsqrt(squares + 1e-05) * norm_ref[...]).astype(BF16)

    def n_copy(q_from, i, device):
        block = normed.at[q_from]
        return send(block, block, n_send.at[i], n_recv.at[i], device)

    n_copy(quarter, 0, at_x).start()
    n_copy(quarter, 1, at_core).start()
    def relay():
        n_copy(q_x, 0, at_x).wait_recv()
        n_copy(q_x, 2, at_core).start()

    split(
        lambda: (
            f_pass(1, 1), f_pass(1, 2), f_pass(1, 3), z_open(2), relay(),
            f_pass(2, 1), f_pass(2, 2), f_pass(2, 3),
        ),
        lambda: (
            f_pass(0, 2), f_pass(0, 3), f_pass(1, 1), relay(), f_pass(1, 2), f_pass(1, 3),
        ),
    )
    for m in range(2):
        for k in range(4):
            f_y_recv(m, k)

    feed_events = {1: lambda: f_pass(2, 1)}

    def feed(i, carry):
        run_events(i, {}, feed_events)

        @pl.when(i == 1)
        def _():
            n_copy(q_core, 1, at_core).wait_recv()

        @pl.when(i == 3)
        def _():
            n_copy(q_diag, 2, at_core).wait_recv()

        slot = base_slot(i)
        tokens = normed[slot]

        def hidden_tile(n, inner_carry):
            lanes = pl.ds(pl.multiple_of(n * tile, 128), tile)
            gate = jnp.dot(tokens, wg[:, :, lanes].reshape(width, tile), preferred_element_type=F32)
            up = jnp.dot(tokens, wu[:, :, lanes].reshape(width, tile), preferred_element_type=F32)
            hidden[slot, :, lanes] = (gate / (1.0 + jnp.exp(-gate)) * up).astype(BF16)
            return inner_carry

        lax.fori_loop(0, units // tile, hidden_tile, 0)
        return carry

    def base_slot(i):
        q = (quarter + 2 * (i // 2)) % 4
        flip = i % 2
        return q + flip * (1 - 2 * (q % 2))

    lax.fori_loop(0, 4, feed, 0)

    def place(j):
        return order(j // 2) * 2 + (y + j) % 2

    def d_copy(i, p):
        if i == 0:
            return send(part.at[q_diag, p], got_core.at[0, p], d_send.at[0, p], d_recv.at[0, p], at_core)
        if i == 1:
            return send(part.at[q_core, p], got_core.at[1, p], d_send.at[1, p], d_recv.at[1, p], at_core)
        return send(to_x.at[p], got_x.at[p], d_send.at[2, p], d_recv.at[2, p], at_x)

    def d_sum(j):
        p = place(j)
        d_copy(0, p).wait_recv()
        to_x[p] = (part[q_x, p].astype(F32) + got_core[0, p].astype(F32)).astype(BF16)
        d_copy(2, p).start()

    def d_done(j):
        p = place(j)
        d_copy(1, p).wait_recv()
        d_copy(2, p).wait_recv()
        lanes = pl.ds(pl.multiple_of(p * rows, 128), rows)
        total = part[quarter, p].astype(F32) + got_core[1, p].astype(F32) + got_x[p].astype(F32)
        result_ref[:, lanes] = (stream[:, lanes].astype(F32) + total).astype(BF16)

    def down(j, carry):
        p = place(j)

        @pl.when(j % 2 == 1)
        def _():
            f_y_recv(2, j // 2)

        value = lax.dot_general(
            hidden[...].reshape(4 * rows, units), wd[p], (((1,), (1,)), ((), ())),
            preferred_element_type=F32,
        )
        value = value.astype(BF16).reshape(4, rows, value.shape[1])
        for g in range(4):
            part[g, p] = value[g]
        d_copy(0, p).start()
        d_copy(1, p).start()

        @pl.when(j >= 1)
        def _():
            d_sum(j - 1)

        @pl.when(j >= 2)
        def _():
            d_done(j - 2)

        run_events(j, {}, {2: lambda: f_pass(2, 2), 4: lambda: f_pass(2, 3)})
        return carry

    lax.fori_loop(0, 8, down, 0)
    d_sum(7)
    d_done(6)
    d_done(7)

    o_core.wait_send()
    o_y().wait_send()
    for group in firsts:
        for copy in group:
            copy.wait_send()
    for k in range(4):
        for s in range(2):
            z_wait_send(o_z(k, s))
        o_x(k).wait_send()
        o_c(k).wait_send()
        for m in range(3):
            for cut in range(2):
                z_wait_send(f_z(m, k, cut))
                f_y(m, k, cut).wait_send()
    n_copy(quarter, 0, at_x).wait_send()
    n_copy(quarter, 1, at_core).wait_send()
    n_copy(q_x, 2, at_core).wait_send()

    def drain(p, carry):
        for i in range(3):
            d_copy(i, p).wait_send()
        return carry

    lax.fori_loop(0, 8, drain, 0)


def per_device_kernel(
    queries, new_kv, cache_pool, page_table, assignment, lengths, lambda_vectors, subln_gain,
    residual, out_weight, norm_gain, gate_weight, up_weight, down_weight_t,
):
    rows, heads, wide = queries.shape
    pages, page_len = cache_pool.shape[:2]
    width, units = residual.shape[1], gate_weight.shape[1] // 4
    keys = pages * page_len + rows
    anyspace = pl.BlockSpec(memory_space=pl.ANY)
    vmem = pl.BlockSpec(memory_space=pltpu.VMEM)
    dma = pltpu.SemaphoreType.DMA
    return pl.pallas_call(
        layer_kernel,
        out_shape=jax.ShapeDtypeStruct((rows, width), BF16),
        in_specs=[pl.BlockSpec(memory_space=pltpu.SMEM)] * 3 + [vmem] * 4 + [anyspace] * 7,
        out_specs=vmem,
        scratch_shapes=[
            pltpu.VMEM((rows, heads, wide), BF16),
            pltpu.VMEM((keys // page_len, page_len, heads, 2 * wide), BF16),
            pltpu.VMEM((heads, rows, wide), BF16),
            pltpu.VMEM((heads, keys, 2 * wide), BF16),
            pltpu.VMEM((rows, width), BF16),
            pltpu.VMEM((4, 2, 256, width), BF16),
            pltpu.VMEM((8, 256, units), BF16),
            pltpu.VMEM((8, 256, units), BF16),
            pltpu.VMEM((8, 256, units), BF16),
            pltpu.VMEM((4, rows, width), BF16),
            pltpu.VMEM((rows, width), BF16),
            pltpu.VMEM((4, rows, units), BF16),
            pltpu.VMEM((4, 8, rows, 256), BF16),
            pltpu.VMEM((2, 8, rows, 256), BF16),
            pltpu.VMEM((8, rows, 256), BF16),
            pltpu.VMEM((8, rows, 256), BF16),
            dma((keys // page_len + 1,)), dma((4,)), dma((3, 3)), dma((3, 3)), dma((3, 2, 10)), dma((3, 2, 10)),
            dma((2, 6)), dma((2, 6)),
            dma((16,)), dma((16,)), dma((3,)), dma((3,)), dma((3, 8)), dma((3, 8)),
        ],
        compiler_params=pltpu.CompilerParams(
            collective_id=0, has_side_effects=True, vmem_limit_bytes=62 * 2**20
        ),
        name="layer",
    )(
        page_table, assignment, lengths, lambda_vectors, subln_gain.reshape(1, -1),
        norm_gain.reshape(1, -1), residual, queries, new_kv, cache_pool,
        out_weight, gate_weight, up_weight, down_weight_t,
    )


def solution(mesh):
    in_specs = (
        P("req", "mlp", None),
        P("req", "mlp", None),
        P("req", None, "mlp", None),
        P("req", None),
        P("req"),
        P(),
        P(),
        P(),
        P("req", "mlp"),
        P("req", "mlp"),
        P(),
        P("req", "mlp"),
        P("req", "mlp"),
        P("req", "mlp"),
    )
    out_specs = P("req", "mlp")
    small = mesh.shape["req"] == 32 and mesh.shape["mlp"] == 1
    return jax.shard_map(
        per_device_kernel if small else per_device, mesh=mesh, in_specs=in_specs, out_specs=out_specs, check_vma=False
    )
```

```python
import jax
import jax.numpy as jnp
from jax import lax
from jax.experimental import pallas as pl
from jax.experimental.pallas import tpu as pltpu
from jax.sharding import PartitionSpec as P

D = 2048


NEG_FILL = -1e30
LAMBDA_BASE = 0.2


def map_block(carried, query_rows, key_half, value_rows, visible, score_scale):
    running_max, running_sum, running_acc = carried
    score = (
        jnp.einsum("nhd,khd->nhk", query_rows, key_half, preferred_element_type=jnp.float32)
        * score_scale
    )
    score = jnp.where(visible[:, None, :], score, NEG_FILL)
    newest = jnp.maximum(running_max, jnp.max(score, axis=2))
    exp_terms = jnp.where(visible[:, None, :], jnp.exp(score - newest[:, :, None]), 0.0)
    shrink = jnp.exp(running_max - newest)
    running_sum = running_sum * shrink + jnp.sum(exp_terms, axis=2)
    running_acc = running_acc * shrink[:, :, None] + jnp.einsum(
        "nhk,khd->nhd",
        exp_terms.astype(jnp.bfloat16),
        value_rows,
        preferred_element_type=jnp.float32,
    )
    return (newest, running_sum, running_acc)


def both_maps(carried, query_rows, key_rows, visible, half_size):
    score_scale = half_size ** (-0.5)
    value_rows = key_rows[:, :, 2 * half_size :]
    map_one = map_block(
        carried[0],
        query_rows[:, :, :half_size],
        key_rows[:, :, :half_size],
        value_rows,
        visible,
        score_scale,
    )
    map_two = map_block(
        carried[1],
        query_rows[:, :, half_size:],
        key_rows[:, :, half_size : 2 * half_size],
        value_rows,
        visible,
        score_scale,
    )
    return (map_one, map_two)


def attend(
    queries, new_kv, cache_pool, page_table, assignment, lengths, lambda_vectors, subln_gain
):
    row_count, head_count, value_width = queries.shape
    half_size = value_width // 2
    page_len = cache_pool.shape[1]
    request = assignment[0]
    cached = jnp.sum(
        jnp.where(jnp.arange(lengths.shape[0], dtype=jnp.int32) == request, lengths, 0)
    )

    def fresh_state():
        return (
            jnp.full((row_count, head_count), NEG_FILL, jnp.float32),
            jnp.zeros((row_count, head_count), jnp.float32),
            jnp.zeros((row_count, head_count, value_width), jnp.float32),
        )

    table_row = page_table[0]

    def page_step(page_index, carried):
        physical = table_row[page_index]
        page_rows = lax.dynamic_index_in_dim(cache_pool, physical, 0, keepdims=False)
        positions = page_index * page_len + jnp.arange(page_len, dtype=jnp.int32)
        visible = jnp.broadcast_to((positions < cached)[None, :], (row_count, page_len))
        return both_maps(carried, queries, page_rows, visible, half_size)

    page_count = (cached + page_len - 1) // page_len
    carried = lax.fori_loop(jnp.int32(0), page_count, page_step, (fresh_state(), fresh_state()))
    token_pos = jnp.arange(row_count, dtype=jnp.int32)
    carried = both_maps(
        carried, queries, new_kv, token_pos[None, :] <= token_pos[:, None], half_size
    )
    lambda_now = (
        jnp.exp(jnp.sum(lambda_vectors[0] * lambda_vectors[1]))
        - jnp.exp(jnp.sum(lambda_vectors[2] * lambda_vectors[3]))
        + LAMBDA_BASE
    )
    mix_out = (
        carried[0][2] / carried[0][1][:, :, None]
        - lambda_now * carried[1][2] / carried[1][1][:, :, None]
    )
    mix_out = (
        mix_out
        * lax.rsqrt(jnp.mean(mix_out * mix_out, axis=2, keepdims=True) + 1e-05)
        * subln_gain
        * (1.0 - LAMBDA_BASE)
    )
    return mix_out.astype(jnp.bfloat16).reshape(row_count, head_count * value_width)


def per_device(
    queries,
    new_kv,
    cache_pool,
    page_table,
    assignment,
    lengths,
    lambda_vectors,
    subln_gain,
    residual,
    out_weight,
    norm_gain,
    gate_weight,
    up_weight,
    down_weight_t,
):
    attn_out = attend(
        queries, new_kv, cache_pool, page_table, assignment, lengths, lambda_vectors, subln_gain
    )
    heads_all = lax.all_gather(attn_out, "mlp", axis=1, tiled=True)
    columns = heads_all
    projected = jnp.dot(
        columns,
        lax.all_gather(out_weight, "req", axis=0, tiled=True),
        preferred_element_type=jnp.float32,
    )
    stream = (residual.astype(jnp.float32) + projected).astype(jnp.bfloat16)
    stream_f = stream.astype(jnp.float32)
    squares = lax.psum(jnp.sum(stream_f * stream_f, axis=1), "mlp")
    slice_width = stream_f.shape[1]
    local_gain = lax.dynamic_slice_in_dim(
        norm_gain, lax.axis_index("mlp") * slice_width, slice_width
    )
    normed_part = (stream_f * lax.rsqrt(squares / D + 1e-05)[:, None] * local_gain).astype(
        jnp.bfloat16
    )
    normed = lax.all_gather(normed_part, "mlp", axis=1, tiled=True)
    columns = normed
    gate_value = jnp.dot(
        columns,
        lax.all_gather(gate_weight, "req", axis=0, tiled=True),
        preferred_element_type=jnp.float32,
    )
    up_value = jnp.dot(
        columns,
        lax.all_gather(up_weight, "req", axis=0, tiled=True),
        preferred_element_type=jnp.float32,
    )
    hidden_act = (jax.nn.silu(gate_value) * up_value).astype(jnp.bfloat16)
    partial_value = lax.dot_general(
        hidden_act,
        lax.all_gather(down_weight_t, "req", axis=0, tiled=True),
        (((1,), (1,)), ((), ())),
        preferred_element_type=jnp.float32,
    )
    summed = lax.psum_scatter(
        partial_value.astype(jnp.bfloat16), "mlp", scatter_dimension=1, tiled=True
    ).astype(jnp.float32)
    return (stream_f + summed).astype(jnp.bfloat16)


BF16, F32 = jnp.bfloat16, jnp.float32
MESH = pl.DeviceIdType.MESH


def layer_kernel(
    table_ref, request_ref, lengths_ref, lambda_ref, gain_ref, norm_ref, residual_ref,
    q_hbm, kv_hbm, pool_hbm, out_hbm, gate_hbm, up_hbm, down_hbm,
    result_ref,
    q_raw, kv_raw, q_buf, kv_buf, attn, wo, wg, wu, wd, normed, stream, hidden, part, got_core, to_x, got_x,
    load_sem, own_sem, first_send, first_recv, far_send, far_recv, oz_send, oz_recv, o_send, o_recv,
    n_send, n_recv, d_send, d_recv,
):
    heads = q_buf.shape[0]
    rows = q_buf.shape[1]
    wide = q_buf.shape[2]
    half = wide // 2
    width = stream.shape[1]
    units = wg.shape[2]
    shard = out_hbm.shape[0]
    halfw = width // 2

    me = lax.axis_index("req")
    core = me % 2
    x = (me // 2) % 2
    quarter = me % 4
    y = (me // 4) % 2
    z = me // 8
    base = me - quarter
    side = z // 2
    inner = z + side * (3 - 2 * z)
    q_core = quarter + 1 - 2 * core
    q_x = (quarter + 2) % 4
    q_diag = (q_core + 2) % 4
    at_core, at_x, at_diag = base + q_core, base + q_x, base + q_diag
    at_y = me + 4 - 8 * y
    off = me - 8 * z
    at_n = off + 8 * (1 + side)
    at_e = off + 8 * (3 * side)
    at_m = off + 8 * (2 - side)
    is_end = inner == 0
    is_mid = inner == 1

    def order(k):
        o = k + inner * (1 - 2 * k) * (1 - k // 2)
        return o + side * (3 - 2 * o)

    def send(src, dst, ssem, rsem, device):
        return pltpu.make_async_remote_copy(
            src_ref=src, dst_ref=dst, send_sem=ssem, recv_sem=rsem,
            device_id={"req": device}, device_id_type=MESH,
        )

    barrier = pltpu.get_barrier_semaphore()

    def greet(device):
        pl.semaphore_signal(barrier, inc=1, device_id={"req": device}, device_id_type=MESH)

    for device in (at_core, at_x, at_diag, at_y):
        greet(device)

    @pl.when(is_end)
    def _():
        greet(at_n)
        pl.semaphore_wait(barrier, 5)

    @pl.when(is_mid)
    def _():
        greet(at_e)
        greet(at_m)
        pl.semaphore_wait(barrier, 6)

    my_half = pl.ds(pl.multiple_of(core * halfw, 128), halfw)
    other_half = pl.ds(pl.multiple_of((1 - core) * halfw, 128), halfw)
    my_rows = pl.ds(pl.multiple_of(quarter * shard, 64), shard)
    core_rows = pl.ds(pl.multiple_of(q_core * shard, 64), shard)
    x_rows = pl.ds(pl.multiple_of(x * 2 * shard, 128), 2 * shard)
    other_x_rows = pl.ds(pl.multiple_of((1 - x) * 2 * shard, 128), 2 * shard)

    o_own = pltpu.make_async_copy(out_hbm.at[:, my_half], wo.at[z, y, my_rows, my_half], own_sem.at[0])
    o_own.start()
    o_core = send(
        out_hbm.at[:, other_half], wo.at[z, y, my_rows, other_half], o_send.at[0], o_recv.at[0], at_core
    )
    o_core.start()

    firsts = []
    owns = []
    for m, (src, dst) in enumerate(((gate_hbm, wg), (up_hbm, wu), (down_hbm, wd))):
        block = dst.at[z * 2 + y, my_rows]
        mine = pltpu.make_async_copy(
            src.at[:, pl.ds(pl.multiple_of(quarter * units, 128), units)], block, own_sem.at[1 + m]
        )
        mine.start()
        owns.append(mine)
        group = []
        for k, (q_to, device) in enumerate(((q_core, at_core), (q_x, at_x), (q_diag, at_diag))):
            copy = send(
                src.at[:, pl.ds(pl.multiple_of(q_to * units, 128), units)],
                block, first_send.at[m, k], first_recv.at[m, k], device,
            )
            copy.start()
            group.append(copy)
        firsts.append(group)

    pages, page_len = pool_hbm.shape[:2]
    chunks = pages + rows // page_len

    q_load = pltpu.make_async_copy(q_hbm, q_raw, load_sem.at[chunks])
    q_load.start()

    def chunk_load(i):
        if i < pages:
            src = pool_hbm.at[i]
        else:
            src = kv_hbm.at[pl.ds((i - pages) * page_len, page_len)]
        return pltpu.make_async_copy(src, kv_raw.at[i], load_sem.at[i])

    for i in range(chunks):
        chunk_load(i).start()

    mats = (wg, wu, wd)

    def along_z(block_at, send_sems, recv_sems, k):
        block = block_at(order(k))

        def to_end(slot):
            return send(block, block, send_sems(slot), recv_sems(slot), at_e)

        def to_mid(slot, at):
            return send(block, block, send_sems(at), recv_sems(slot), at_m)

        if k == 0:
            return (
                [send(block, block, send_sems(1), recv_sems(1), at_n)],
                [to_end(1), to_mid(2, 4)],
            )
        if k == 1:
            return [], [to_mid(3, 5)]
        return [], [to_end(k)]

    def z_start(copies):
        for_end, for_mid = copies
        if for_end:
            @pl.when(is_end)
            def _():
                for copy in for_end:
                    copy.start()

        @pl.when(is_mid)
        def _():
            for copy in for_mid:
                copy.start()

    def z_wait_send(copies):
        for_end, for_mid = copies
        if for_end:
            @pl.when(is_end)
            def _():
                for copy in for_end:
                    copy.wait_send()

        @pl.when(is_mid)
        def _():
            for copy in for_mid:
                copy.wait_send()

    def f_block(m, part):
        span = pl.ds(part * (mats[m].shape[1] // 2), mats[m].shape[1] // 2)
        return lambda zz: mats[m].at[zz * 2 + y, span]

    def f_z(m, k, part):
        return along_z(
            f_block(m, part),
            lambda i: far_send.at[m, part, i],
            lambda i: far_recv.at[m, part, i],
            k,
        )

    def f_z_recv(m, k, part):
        block = f_block(m, part)(order(k))
        send(block, block, far_send.at[m, part, k], far_recv.at[m, part, k], at_y).wait_recv()

    def f_y(m, k, part):
        block = f_block(m, part)(order(k))
        return send(block, block, far_send.at[m, part, 6 + k], far_recv.at[m, part, 6 + k], at_y)

    def f_y_recv(m, k):
        for part in range(2):
            half_rows = mats[m].shape[1] // 2
            block = mats[m].at[order(k) * 2 + 1 - y, pl.ds(part * half_rows, half_rows)]
            send(
                block, block, far_send.at[m, part, 6 + k], far_recv.at[m, part, 6 + k], at_y
            ).wait_recv()

    def f_first(m):
        owns[m].wait()
        for i, q_from in enumerate((q_core, q_x, q_diag)):
            block = mats[m].at[z * 2 + y, pl.ds(pl.multiple_of(q_from * shard, 64), shard)]
            send(block, block, first_send.at[m, i], first_recv.at[m, i], at_core).wait_recv()
        for part in range(2):
            f_y(m, 0, part).start()

    def f_pass(m, k):
        for part in range(2):
            f_z_recv(m, k, part)
            z_start(f_z(m, k, part))
            f_y(m, k, part).start()

    def o_block(s):
        return lambda zz: wo.at[zz, (y + s) % 2, x_rows, my_half]

    def o_z(k, s):
        return along_z(o_block(s), lambda i: oz_send.at[s, i], lambda i: oz_recv.at[s, i], k)

    def o_x(k):
        block = wo.at[order(k), :, x_rows, my_half]
        return send(block, block, o_send.at[8 + k], o_recv.at[8 + k], at_x)

    def o_c(k):
        block = wo.at[order(k), :, :, my_half]
        return send(block, block, o_send.at[12 + k], o_recv.at[12 + k], at_core)

    def o_y():
        block = wo.at[z, y, x_rows, my_half]
        return send(block, block, o_send.at[1], o_recv.at[1], at_y)

    def o_first():
        o_own.wait()
        block = wo.at[z, y, core_rows, my_half]
        send(block, block, o_send.at[0], o_recv.at[0], at_core).wait_recv()
        z_start(o_z(0, 0))
        o_y().start()

    def o_second():
        block = wo.at[z, 1 - y, x_rows, my_half]
        send(block, block, o_send.at[1], o_recv.at[1], at_y).wait_recv()
        z_start(o_z(0, 1))
        o_x(0).start()

    def o_pass(k):
        for s in range(2):
            block = o_block(s)(order(k))
            send(block, block, oz_send.at[s, k], oz_recv.at[s, k], at_y).wait_recv()
            z_start(o_z(k, s))
        o_x(k).start()

    def o_share(k):
        block = wo.at[order(k), :, other_x_rows, my_half]
        send(block, block, o_send.at[8 + k], o_recv.at[8 + k], at_x).wait_recv()
        o_c(k).start()

    def o_shared(k):
        block = wo.at[order(k), :, :, other_half]
        send(block, block, o_send.at[12 + k], o_recv.at[12 + k], at_core).wait_recv()

    def z_open(m):
        for part in range(2):
            z_start(f_z(m, 0, part))

    def split(at_mid, at_end):
        @pl.when(is_mid)
        def _():
            at_mid()

        @pl.when(is_end)
        def _():
            at_end()

    def run_events(step, at_mid, at_end):
        for place_at, events in ((is_mid, at_mid), (is_end, at_end)):
            for i, event in events.items():
                @pl.when(jnp.logical_and(place_at, step == i))
                def _(event=event):
                    event()

    o_first()

    q_load.wait()
    for i in range(rows // page_len):
        span = pl.ds(i * page_len, page_len)
        q_buf[:, span, :] = jnp.swapaxes(q_raw[span], 0, 1)

    chunk_events = {1: o_second, 3: lambda: f_first(0), 5: lambda: f_first(1), 7: lambda: f_first(2)}

    def turn(i, carry):
        pltpu.make_async_copy(pool_hbm.at[0], kv_raw.at[i], load_sem.at[i]).wait()
        span = pl.ds(pl.multiple_of(i * page_len, page_len), page_len)
        kv_buf[:, span, :] = jnp.swapaxes(kv_raw[i], 0, 1)
        run_events(i, chunk_events, chunk_events)
        return carry

    lax.fori_loop(0, chunks, turn, 0)

    mid_events = {
        2: lambda: (o_pass(2), o_pass(1)),
        3: lambda: (o_share(0), z_open(0)),
        5: lambda: o_pass(3),
        6: lambda: (o_share(1), z_open(1), f_pass(0, 1)),
        7: lambda: (f_pass(0, 2), f_pass(1, 1)),
    }
    end_events = {
        2: lambda: z_open(0),
        3: lambda: (o_pass(1), o_share(0)),
        4: lambda: z_open(1),
        6: lambda: (o_share(1), z_open(2)),
        7: lambda: o_pass(2),
    }

    vectors = lambda_ref[...]
    lam = (
        jnp.exp(jnp.sum(vectors[0:1] * vectors[1:2], axis=1, keepdims=True))
        - jnp.exp(jnp.sum(vectors[2:3] * vectors[3:4], axis=1, keepdims=True))
        + LAMBDA_BASE
    )
    length = lengths_ref[request_ref[0]]
    within = lax.broadcasted_iota(jnp.int32, (1, page_len), 1)
    pieces = []
    for page in range(pages):
        logical = jnp.int32(0)
        for j in range(pages):
            logical = logical + jnp.where(table_ref[0, j] == page, j, 0)
        pieces.append(jnp.where(within + logical * page_len < length, 0.0, NEG_FILL))
    bias = jnp.concatenate(pieces, axis=1).astype(F32)
    causal = jnp.where(
        lax.broadcasted_iota(jnp.int32, (rows, rows), 1)
        <= lax.broadcasted_iota(jnp.int32, (rows, rows), 0),
        0.0,
        NEG_FILL,
    ).astype(F32)

    def head_step(h, carry):
        values = kv_buf[h, :, wide:]
        mixed = []
        for one in range(2):
            lanes = slice(one * half, (one + 1) * half)
            score = lax.dot_general(
                q_buf[h, :, lanes], kv_buf[h, :, lanes], (((1,), (1,)), ((), ())),
                preferred_element_type=F32,
            ) * (half ** -0.5)
            cached = bias.shape[1]
            score = jnp.concatenate(
                [score[:, :cached] + bias, score[:, cached:] + causal], axis=1
            )
            expo = jnp.exp(score - jnp.max(score, axis=1, keepdims=True))
            total = jnp.sum(expo, axis=1, keepdims=True)
            mixed.append(jnp.dot(expo.astype(BF16), values, preferred_element_type=F32) / total)
        mix = mixed[0] - lam * mixed[1]
        mix = mix * lax.rsqrt(jnp.mean(mix * mix, axis=1, keepdims=True) + 1e-05)
        mix = mix * gain_ref[...] * (1.0 - LAMBDA_BASE)
        attn[:, pl.ds(pl.multiple_of(h * wide, 128), wide)] = mix.astype(BF16)
        run_events(h, mid_events, end_events)
        return carry

    lax.fori_loop(0, heads, head_step, 0)

    split(
        lambda: (
            o_share(2), f_pass(0, 3), f_pass(1, 2), f_pass(1, 3), o_share(3), z_open(2),
            f_pass(2, 1), f_pass(2, 2),
        ),
        lambda: (
            f_pass(0, 1), o_share(2), o_pass(3), f_pass(1, 1), f_pass(0, 2), o_share(3),
            f_pass(0, 3),
        ),
    )
    for k in range(4):
        o_shared(k)

    tile = 2 * half

    def project(n, carry):
        lanes = pl.ds(pl.multiple_of(n * tile, 128), tile)
        weight = wo[:, :, :, lanes].reshape(width, tile)
        value = jnp.dot(attn[...], weight, preferred_element_type=F32)
        stream[:, lanes] = (residual_ref[:, lanes].astype(F32) + value).astype(BF16)
        return carry

    lax.fori_loop(0, width // tile, project, 0)
    stream_f = stream[...].astype(F32)
    squares = jnp.mean(stream_f * stream_f, axis=1, keepdims=True)
    normed[quarter] = (stream_f * lax.rsqrt(squares + 1e-05) * norm_ref[...]).astype(BF16)

    def n_copy(q_from, i, device):
        block = normed.at[q_from]
        return send(block, block, n_send.at[i], n_recv.at[i], device)

    n_copy(quarter, 0, at_x).start()
    n_copy(quarter, 1, at_core).start()
    def relay():
        n_copy(q_x, 0, at_x).wait_recv()
        n_copy(q_x, 2, at_core).start()

    split(
        lambda: f_pass(2, 3),
        lambda: (f_pass(1, 2), f_pass(1, 3), f_pass(2, 1)),
    )
    for m in range(2):
        for k in range(4):
            f_y_recv(m, k)

    feed_events = {1: lambda: f_pass(2, 2), 3: lambda: f_pass(2, 3)}

    def feed(i, carry):
        run_events(i, {}, feed_events)

        @pl.when(i == 1)
        def _():
            n_copy(q_core, 1, at_core).wait_recv()

        @pl.when(i == 2)
        def _():
            relay()

        @pl.when(i == 3)
        def _():
            n_copy(q_diag, 2, at_core).wait_recv()

        slot = base_slot(i)
        tokens = normed[slot]

        def hidden_tile(n, inner_carry):
            lanes = pl.ds(pl.multiple_of(n * tile, 128), tile)
            gate = jnp.dot(tokens, wg[:, :, lanes].reshape(width, tile), preferred_element_type=F32)
            up = jnp.dot(tokens, wu[:, :, lanes].reshape(width, tile), preferred_element_type=F32)
            hidden[slot, :, lanes] = (gate / (1.0 + jnp.exp(-gate)) * up).astype(BF16)
            return inner_carry

        lax.fori_loop(0, units // tile, hidden_tile, 0)
        return carry

    def base_slot(i):
        q = (quarter + 2 * (i // 2)) % 4
        flip = i % 2
        return q + flip * (1 - 2 * (q % 2))

    lax.fori_loop(0, 4, feed, 0)

    def place(j):
        return order(j // 2) * 2 + (y + j) % 2

    def d_copy(i, p):
        if i == 0:
            return send(part.at[q_diag, p], got_core.at[0, p], d_send.at[0, p], d_recv.at[0, p], at_core)
        if i == 1:
            return send(part.at[q_core, p], got_core.at[1, p], d_send.at[1, p], d_recv.at[1, p], at_core)
        return send(to_x.at[p], got_x.at[p], d_send.at[2, p], d_recv.at[2, p], at_x)

    def d_sum(j):
        p = place(j)
        d_copy(0, p).wait_recv()
        to_x[p] = (part[q_x, p].astype(F32) + got_core[0, p].astype(F32)).astype(BF16)
        d_copy(2, p).start()

    def d_done(j):
        p = place(j)
        d_copy(1, p).wait_recv()
        d_copy(2, p).wait_recv()
        lanes = pl.ds(pl.multiple_of(p * rows, 128), rows)
        total = part[quarter, p].astype(F32) + got_core[1, p].astype(F32) + got_x[p].astype(F32)
        result_ref[:, lanes] = (stream[:, lanes].astype(F32) + total).astype(BF16)

    def down(j, carry):
        p = place(j)

        @pl.when(j % 2 == 1)
        def _():
            f_y_recv(2, j // 2)

        value = lax.dot_general(
            hidden[...].reshape(4 * rows, units), wd[p], (((1,), (1,)), ((), ())),
            preferred_element_type=F32,
        )
        value = value.astype(BF16).reshape(4, rows, value.shape[1])
        for g in range(4):
            part[g, p] = value[g]
        d_copy(0, p).start()
        d_copy(1, p).start()

        @pl.when(j >= 1)
        def _():
            d_sum(j - 1)

        @pl.when(j >= 2)
        def _():
            d_done(j - 2)

        return carry

    lax.fori_loop(0, 8, down, 0)
    d_sum(7)
    d_done(6)
    d_done(7)

    o_core.wait_send()
    o_y().wait_send()
    for group in firsts:
        for copy in group:
            copy.wait_send()
    for k in range(4):
        for s in range(2):
            z_wait_send(o_z(k, s))
        o_x(k).wait_send()
        o_c(k).wait_send()
        for m in range(3):
            for cut in range(2):
                z_wait_send(f_z(m, k, cut))
                f_y(m, k, cut).wait_send()
    n_copy(quarter, 0, at_x).wait_send()
    n_copy(quarter, 1, at_core).wait_send()
    n_copy(q_x, 2, at_core).wait_send()

    def drain(p, carry):
        for i in range(3):
            d_copy(i, p).wait_send()
        return carry

    lax.fori_loop(0, 8, drain, 0)


def per_device_kernel(
    queries, new_kv, cache_pool, page_table, assignment, lengths, lambda_vectors, subln_gain,
    residual, out_weight, norm_gain, gate_weight, up_weight, down_weight_t,
):
    rows, heads, wide = queries.shape
    pages, page_len = cache_pool.shape[:2]
    width, units = residual.shape[1], gate_weight.shape[1] // 4
    keys = pages * page_len + rows
    anyspace = pl.BlockSpec(memory_space=pl.ANY)
    vmem = pl.BlockSpec(memory_space=pltpu.VMEM)
    dma = pltpu.SemaphoreType.DMA
    return pl.pallas_call(
        layer_kernel,
        out_shape=jax.ShapeDtypeStruct((rows, width), BF16),
        in_specs=[pl.BlockSpec(memory_space=pltpu.SMEM)] * 3 + [vmem] * 4 + [anyspace] * 7,
        out_specs=vmem,
        scratch_shapes=[
            pltpu.VMEM((rows, heads, wide), BF16),
            pltpu.VMEM((keys // page_len, page_len, heads, 2 * wide), BF16),
            pltpu.VMEM((heads, rows, wide), BF16),
            pltpu.VMEM((heads, keys, 2 * wide), BF16),
            pltpu.VMEM((rows, width), BF16),
            pltpu.VMEM((4, 2, 256, width), BF16),
            pltpu.VMEM((8, 256, units), BF16),
            pltpu.VMEM((8, 256, units), BF16),
            pltpu.VMEM((8, 256, units), BF16),
            pltpu.VMEM((4, rows, width), BF16),
            pltpu.VMEM((rows, width), BF16),
            pltpu.VMEM((4, rows, units), BF16),
            pltpu.VMEM((4, 8, rows, 256), BF16),
            pltpu.VMEM((2, 8, rows, 256), BF16),
            pltpu.VMEM((8, rows, 256), BF16),
            pltpu.VMEM((8, rows, 256), BF16),
            dma((keys // page_len + 1,)), dma((4,)), dma((3, 3)), dma((3, 3)), dma((3, 2, 10)), dma((3, 2, 10)),
            dma((2, 6)), dma((2, 6)),
            dma((16,)), dma((16,)), dma((3,)), dma((3,)), dma((3, 8)), dma((3, 8)),
        ],
        compiler_params=pltpu.CompilerParams(
            collective_id=0, has_side_effects=True, vmem_limit_bytes=62 * 2**20
        ),
        name="layer",
    )(
        page_table, assignment, lengths, lambda_vectors, subln_gain.reshape(1, -1),
        norm_gain.reshape(1, -1), residual, queries, new_kv, cache_pool,
        out_weight, gate_weight, up_weight, down_weight_t,
    )


def solution(mesh):
    in_specs = (
        P("req", "mlp", None),
        P("req", "mlp", None),
        P("req", None, "mlp", None),
        P("req", None),
        P("req"),
        P(),
        P(),
        P(),
        P("req", "mlp"),
        P("req", "mlp"),
        P(),
        P("req", "mlp"),
        P("req", "mlp"),
        P("req", "mlp"),
    )
    out_specs = P("req", "mlp")
    small = mesh.shape["req"] == 32 and mesh.shape["mlp"] == 1
    return jax.shard_map(
        per_device_kernel if small else per_device, mesh=mesh, in_specs=in_specs, out_specs=out_specs, check_vma=False
    )
```

```python
import jax
import jax.numpy as jnp
from jax import lax
from jax.experimental import pallas as pl
from jax.experimental.pallas import tpu as pltpu
from jax.sharding import PartitionSpec as P

D = 2048


NEG_FILL = -1e30
LAMBDA_BASE = 0.2


def map_block(carried, query_rows, key_half, value_rows, visible, score_scale):
    running_max, running_sum, running_acc = carried
    score = (
        jnp.einsum("nhd,khd->nhk", query_rows, key_half, preferred_element_type=jnp.float32)
        * score_scale
    )
    score = jnp.where(visible[:, None, :], score, NEG_FILL)
    newest = jnp.maximum(running_max, jnp.max(score, axis=2))
    exp_terms = jnp.where(visible[:, None, :], jnp.exp(score - newest[:, :, None]), 0.0)
    shrink = jnp.exp(running_max - newest)
    running_sum = running_sum * shrink + jnp.sum(exp_terms, axis=2)
    running_acc = running_acc * shrink[:, :, None] + jnp.einsum(
        "nhk,khd->nhd",
        exp_terms.astype(jnp.bfloat16),
        value_rows,
        preferred_element_type=jnp.float32,
    )
    return (newest, running_sum, running_acc)


def both_maps(carried, query_rows, key_rows, visible, half_size):
    score_scale = half_size ** (-0.5)
    value_rows = key_rows[:, :, 2 * half_size :]
    map_one = map_block(
        carried[0],
        query_rows[:, :, :half_size],
        key_rows[:, :, :half_size],
        value_rows,
        visible,
        score_scale,
    )
    map_two = map_block(
        carried[1],
        query_rows[:, :, half_size:],
        key_rows[:, :, half_size : 2 * half_size],
        value_rows,
        visible,
        score_scale,
    )
    return (map_one, map_two)


def attend(
    queries, new_kv, cache_pool, page_table, assignment, lengths, lambda_vectors, subln_gain
):
    row_count, head_count, value_width = queries.shape
    half_size = value_width // 2
    page_len = cache_pool.shape[1]
    request = assignment[0]
    cached = jnp.sum(
        jnp.where(jnp.arange(lengths.shape[0], dtype=jnp.int32) == request, lengths, 0)
    )

    def fresh_state():
        return (
            jnp.full((row_count, head_count), NEG_FILL, jnp.float32),
            jnp.zeros((row_count, head_count), jnp.float32),
            jnp.zeros((row_count, head_count, value_width), jnp.float32),
        )

    table_row = page_table[0]

    def page_step(page_index, carried):
        physical = table_row[page_index]
        page_rows = lax.dynamic_index_in_dim(cache_pool, physical, 0, keepdims=False)
        positions = page_index * page_len + jnp.arange(page_len, dtype=jnp.int32)
        visible = jnp.broadcast_to((positions < cached)[None, :], (row_count, page_len))
        return both_maps(carried, queries, page_rows, visible, half_size)

    page_count = (cached + page_len - 1) // page_len
    carried = lax.fori_loop(jnp.int32(0), page_count, page_step, (fresh_state(), fresh_state()))
    token_pos = jnp.arange(row_count, dtype=jnp.int32)
    carried = both_maps(
        carried, queries, new_kv, token_pos[None, :] <= token_pos[:, None], half_size
    )
    lambda_now = (
        jnp.exp(jnp.sum(lambda_vectors[0] * lambda_vectors[1]))
        - jnp.exp(jnp.sum(lambda_vectors[2] * lambda_vectors[3]))
        + LAMBDA_BASE
    )
    mix_out = (
        carried[0][2] / carried[0][1][:, :, None]
        - lambda_now * carried[1][2] / carried[1][1][:, :, None]
    )
    mix_out = (
        mix_out
        * lax.rsqrt(jnp.mean(mix_out * mix_out, axis=2, keepdims=True) + 1e-05)
        * subln_gain
        * (1.0 - LAMBDA_BASE)
    )
    return mix_out.astype(jnp.bfloat16).reshape(row_count, head_count * value_width)


def per_device(
    queries,
    new_kv,
    cache_pool,
    page_table,
    assignment,
    lengths,
    lambda_vectors,
    subln_gain,
    residual,
    out_weight,
    norm_gain,
    gate_weight,
    up_weight,
    down_weight_t,
):
    attn_out = attend(
        queries, new_kv, cache_pool, page_table, assignment, lengths, lambda_vectors, subln_gain
    )
    heads_all = lax.all_gather(attn_out, "mlp", axis=1, tiled=True)
    columns = heads_all
    projected = jnp.dot(
        columns,
        lax.all_gather(out_weight, "req", axis=0, tiled=True),
        preferred_element_type=jnp.float32,
    )
    stream = (residual.astype(jnp.float32) + projected).astype(jnp.bfloat16)
    stream_f = stream.astype(jnp.float32)
    squares = lax.psum(jnp.sum(stream_f * stream_f, axis=1), "mlp")
    slice_width = stream_f.shape[1]
    local_gain = lax.dynamic_slice_in_dim(
        norm_gain, lax.axis_index("mlp") * slice_width, slice_width
    )
    normed_part = (stream_f * lax.rsqrt(squares / D + 1e-05)[:, None] * local_gain).astype(
        jnp.bfloat16
    )
    normed = lax.all_gather(normed_part, "mlp", axis=1, tiled=True)
    columns = normed
    gate_value = jnp.dot(
        columns,
        lax.all_gather(gate_weight, "req", axis=0, tiled=True),
        preferred_element_type=jnp.float32,
    )
    up_value = jnp.dot(
        columns,
        lax.all_gather(up_weight, "req", axis=0, tiled=True),
        preferred_element_type=jnp.float32,
    )
    hidden_act = (jax.nn.silu(gate_value) * up_value).astype(jnp.bfloat16)
    partial_value = lax.dot_general(
        hidden_act,
        lax.all_gather(down_weight_t, "req", axis=0, tiled=True),
        (((1,), (1,)), ((), ())),
        preferred_element_type=jnp.float32,
    )
    summed = lax.psum_scatter(
        partial_value.astype(jnp.bfloat16), "mlp", scatter_dimension=1, tiled=True
    ).astype(jnp.float32)
    return (stream_f + summed).astype(jnp.bfloat16)


BF16, F32 = jnp.bfloat16, jnp.float32
MESH = pl.DeviceIdType.MESH


def layer_kernel(
    table_ref, request_ref, lengths_ref, lambda_ref, gain_ref, norm_ref, residual_ref,
    q_hbm, kv_hbm, pool_hbm, out_hbm, gate_hbm, up_hbm, down_hbm,
    result_ref,
    q_raw, kv_raw, q_buf, kv_buf, attn, wo, wg, wu, wd, normed, stream, hidden, part, got_core, to_x, got_x,
    load_sem, own_sem, first_send, first_recv, far_send, far_recv, oz_send, oz_recv, o_send, o_recv,
    n_send, n_recv, d_send, d_recv,
):
    heads = q_buf.shape[0]
    rows = q_buf.shape[1]
    wide = q_buf.shape[2]
    half = wide // 2
    width = stream.shape[1]
    units = wg.shape[2]
    shard = out_hbm.shape[0]
    halfw = width // 2

    me = lax.axis_index("req")
    core = me % 2
    x = (me // 2) % 2
    quarter = me % 4
    y = (me // 4) % 2
    z = me // 8
    base = me - quarter
    side = z // 2
    inner = z + side * (3 - 2 * z)
    q_core = quarter + 1 - 2 * core
    q_x = (quarter + 2) % 4
    q_diag = (q_core + 2) % 4
    at_core, at_x, at_diag = base + q_core, base + q_x, base + q_diag
    at_y = me + 4 - 8 * y
    off = me - 8 * z
    at_n = off + 8 * (1 + side)
    at_e = off + 8 * (3 * side)
    at_m = off + 8 * (2 - side)
    is_end = inner == 0
    is_mid = inner == 1

    def order(k):
        o = k + inner * (1 - 2 * k) * (1 - k // 2)
        return o + side * (3 - 2 * o)

    def send(src, dst, ssem, rsem, device):
        return pltpu.make_async_remote_copy(
            src_ref=src, dst_ref=dst, send_sem=ssem, recv_sem=rsem,
            device_id={"req": device}, device_id_type=MESH,
        )

    barrier = pltpu.get_barrier_semaphore()

    def greet(device):
        pl.semaphore_signal(barrier, inc=1, device_id={"req": device}, device_id_type=MESH)

    for device in (at_core, at_x, at_diag, at_y):
        greet(device)

    @pl.when(is_end)
    def _():
        greet(at_n)
        pl.semaphore_wait(barrier, 5)

    @pl.when(is_mid)
    def _():
        greet(at_e)
        greet(at_m)
        pl.semaphore_wait(barrier, 6)

    my_half = pl.ds(pl.multiple_of(core * halfw, 128), halfw)
    other_half = pl.ds(pl.multiple_of((1 - core) * halfw, 128), halfw)
    my_rows = pl.ds(pl.multiple_of(quarter * shard, 64), shard)
    core_rows = pl.ds(pl.multiple_of(q_core * shard, 64), shard)
    x_rows = pl.ds(pl.multiple_of(x * 2 * shard, 128), 2 * shard)
    other_x_rows = pl.ds(pl.multiple_of((1 - x) * 2 * shard, 128), 2 * shard)

    o_own = pltpu.make_async_copy(out_hbm.at[:, my_half], wo.at[z, y, my_rows, my_half], own_sem.at[0])
    o_own.start()
    o_core = send(
        out_hbm.at[:, other_half], wo.at[z, y, my_rows, other_half], o_send.at[0], o_recv.at[0], at_core
    )
    o_core.start()

    firsts = []
    owns = []
    for m, (src, dst) in enumerate(((gate_hbm, wg), (up_hbm, wu), (down_hbm, wd))):
        block = dst.at[z * 2 + y, my_rows]
        mine = pltpu.make_async_copy(
            src.at[:, pl.ds(pl.multiple_of(quarter * units, 128), units)], block, own_sem.at[1 + m]
        )
        mine.start()
        owns.append(mine)
        group = []
        for k, (q_to, device) in enumerate(((q_core, at_core), (q_x, at_x), (q_diag, at_diag))):
            copy = send(
                src.at[:, pl.ds(pl.multiple_of(q_to * units, 128), units)],
                block, first_send.at[m, k], first_recv.at[m, k], device,
            )
            copy.start()
            group.append(copy)
        firsts.append(group)

    pages, page_len = pool_hbm.shape[:2]
    chunks = pages + rows // page_len

    q_load = pltpu.make_async_copy(q_hbm, q_raw, load_sem.at[chunks])
    q_load.start()

    def chunk_load(i):
        if i < pages:
            src = pool_hbm.at[i]
        else:
            src = kv_hbm.at[pl.ds((i - pages) * page_len, page_len)]
        return pltpu.make_async_copy(src, kv_raw.at[i], load_sem.at[i])

    for i in range(chunks):
        chunk_load(i).start()

    mats = (wg, wu, wd)

    def along_z(block_at, send_sems, recv_sems, k):
        block = block_at(order(k))

        def to_end(slot):
            return send(block, block, send_sems(slot), recv_sems(slot), at_e)

        def to_mid(slot, at):
            return send(block, block, send_sems(at), recv_sems(slot), at_m)

        if k == 0:
            return (
                [send(block, block, send_sems(1), recv_sems(1), at_n)],
                [to_end(1), to_mid(2, 4)],
            )
        if k == 1:
            return [], [to_mid(3, 5)]
        return [], [to_end(k)]

    def z_start(copies):
        for_end, for_mid = copies
        if for_end:
            @pl.when(is_end)
            def _():
                for copy in for_end:
                    copy.start()

        @pl.when(is_mid)
        def _():
            for copy in for_mid:
                copy.start()

    def z_wait_send(copies):
        for_end, for_mid = copies
        if for_end:
            @pl.when(is_end)
            def _():
                for copy in for_end:
                    copy.wait_send()

        @pl.when(is_mid)
        def _():
            for copy in for_mid:
                copy.wait_send()

    def f_block(m, part):
        span = pl.ds(part * (mats[m].shape[1] // 2), mats[m].shape[1] // 2)
        return lambda zz: mats[m].at[zz * 2 + y, span]

    def f_z(m, k, part):
        return along_z(
            f_block(m, part),
            lambda i: far_send.at[m, part, i],
            lambda i: far_recv.at[m, part, i],
            k,
        )

    def f_z_recv(m, k, part):
        block = f_block(m, part)(order(k))
        send(block, block, far_send.at[m, part, k], far_recv.at[m, part, k], at_y).wait_recv()

    def f_y(m, k, part):
        block = f_block(m, part)(order(k))
        return send(block, block, far_send.at[m, part, 6 + k], far_recv.at[m, part, 6 + k], at_y)

    def f_y_recv(m, k):
        for part in range(2):
            half_rows = mats[m].shape[1] // 2
            block = mats[m].at[order(k) * 2 + 1 - y, pl.ds(part * half_rows, half_rows)]
            send(
                block, block, far_send.at[m, part, 6 + k], far_recv.at[m, part, 6 + k], at_y
            ).wait_recv()

    def f_first(m):
        owns[m].wait()
        for i, q_from in enumerate((q_core, q_x, q_diag)):
            block = mats[m].at[z * 2 + y, pl.ds(pl.multiple_of(q_from * shard, 64), shard)]
            send(block, block, first_send.at[m, i], first_recv.at[m, i], at_core).wait_recv()
        for part in range(2):
            f_y(m, 0, part).start()

    def f_pass(m, k):
        for part in range(2):
            f_z_recv(m, k, part)
            z_start(f_z(m, k, part))
            f_y(m, k, part).start()

    def o_block(s):
        return lambda zz: wo.at[zz, (y + s) % 2, x_rows, my_half]

    def o_z(k, s):
        return along_z(o_block(s), lambda i: oz_send.at[s, i], lambda i: oz_recv.at[s, i], k)

    def o_x(k):
        block = wo.at[order(k), :, x_rows, my_half]
        return send(block, block, o_send.at[8 + k], o_recv.at[8 + k], at_x)

    def o_c(k):
        block = wo.at[order(k), :, :, my_half]
        return send(block, block, o_send.at[12 + k], o_recv.at[12 + k], at_core)

    def o_y():
        block = wo.at[z, y, x_rows, my_half]
        return send(block, block, o_send.at[1], o_recv.at[1], at_y)

    def o_first():
        o_own.wait()
        block = wo.at[z, y, core_rows, my_half]
        send(block, block, o_send.at[0], o_recv.at[0], at_core).wait_recv()
        z_start(o_z(0, 0))
        o_y().start()

    def o_second():
        block = wo.at[z, 1 - y, x_rows, my_half]
        send(block, block, o_send.at[1], o_recv.at[1], at_y).wait_recv()
        z_start(o_z(0, 1))
        o_x(0).start()

    def o_pass(k):
        for s in range(2):
            block = o_block(s)(order(k))
            send(block, block, oz_send.at[s, k], oz_recv.at[s, k], at_y).wait_recv()
            z_start(o_z(k, s))
        o_x(k).start()

    def o_share(k):
        block = wo.at[order(k), :, other_x_rows, my_half]
        send(block, block, o_send.at[8 + k], o_recv.at[8 + k], at_x).wait_recv()
        o_c(k).start()

    def o_shared(k):
        block = wo.at[order(k), :, :, other_half]
        send(block, block, o_send.at[12 + k], o_recv.at[12 + k], at_core).wait_recv()

    def z_open(m):
        for part in range(2):
            z_start(f_z(m, 0, part))

    def split(at_mid, at_end):
        @pl.when(is_mid)
        def _():
            at_mid()

        @pl.when(is_end)
        def _():
            at_end()

    def run_events(step, at_mid, at_end):
        for place_at, events in ((is_mid, at_mid), (is_end, at_end)):
            for i, event in events.items():
                @pl.when(jnp.logical_and(place_at, step == i))
                def _(event=event):
                    event()

    o_first()

    q_load.wait()
    for i in range(rows // page_len):
        span = pl.ds(i * page_len, page_len)
        q_buf[:, span, :] = jnp.swapaxes(q_raw[span], 0, 1)

    both_chunk = {
        0: o_second, 1: lambda: f_first(0), 2: lambda: f_first(1), 3: lambda: f_first(2),
        5: lambda: (o_share(0), z_open(0)),
    }
    mid_chunk = both_chunk | {
        4: lambda: (o_pass(2), o_pass(1)), 7: lambda: (o_pass(3), z_open(1))
    }
    end_chunk = both_chunk | {6: lambda: (o_pass(1), z_open(1))}

    def turn(i, carry):
        pltpu.make_async_copy(pool_hbm.at[0], kv_raw.at[i], load_sem.at[i]).wait()
        span = pl.ds(pl.multiple_of(i * page_len, page_len), page_len)
        kv_buf[:, span, :] = jnp.swapaxes(kv_raw[i], 0, 1)
        run_events(i, mid_chunk, end_chunk)
        return carry

    lax.fori_loop(0, chunks, turn, 0)

    mid_events = {
        0: lambda: o_share(1),
        1: lambda: f_pass(0, 1),
        2: lambda: f_pass(0, 2),
        3: lambda: f_pass(1, 1),
        4: lambda: (o_share(2), f_pass(0, 3)),
        5: lambda: f_pass(1, 2),
        6: lambda: (f_pass(1, 3), o_share(3)),
        7: lambda: z_open(2),
    }
    end_events = {
        0: lambda: o_share(1),
        1: lambda: (o_pass(2), z_open(2)),
        2: lambda: f_pass(0, 1),
        4: lambda: o_share(2),
        5: lambda: o_pass(3),
        6: lambda: (f_pass(1, 1), f_pass(0, 2)),
        7: lambda: o_share(3),
    }

    vectors = lambda_ref[...]
    lam = (
        jnp.exp(jnp.sum(vectors[0:1] * vectors[1:2], axis=1, keepdims=True))
        - jnp.exp(jnp.sum(vectors[2:3] * vectors[3:4], axis=1, keepdims=True))
        + LAMBDA_BASE
    )
    length = lengths_ref[request_ref[0]]
    within = lax.broadcasted_iota(jnp.int32, (1, page_len), 1)
    pieces = []
    for page in range(pages):
        logical = jnp.int32(0)
        for j in range(pages):
            logical = logical + jnp.where(table_ref[0, j] == page, j, 0)
        pieces.append(jnp.where(within + logical * page_len < length, 0.0, NEG_FILL))
    bias = jnp.concatenate(pieces, axis=1).astype(F32)
    causal = jnp.where(
        lax.broadcasted_iota(jnp.int32, (rows, rows), 1)
        <= lax.broadcasted_iota(jnp.int32, (rows, rows), 0),
        0.0,
        NEG_FILL,
    ).astype(F32)

    def head_step(h, carry):
        values = kv_buf[h, :, wide:]
        mixed = []
        for one in range(2):
            lanes = slice(one * half, (one + 1) * half)
            score = lax.dot_general(
                q_buf[h, :, lanes], kv_buf[h, :, lanes], (((1,), (1,)), ((), ())),
                preferred_element_type=F32,
            ) * (half ** -0.5)
            cached = bias.shape[1]
            score = jnp.concatenate(
                [score[:, :cached] + bias, score[:, cached:] + causal], axis=1
            )
            expo = jnp.exp(score - jnp.max(score, axis=1, keepdims=True))
            total = jnp.sum(expo, axis=1, keepdims=True)
            mixed.append(jnp.dot(expo.astype(BF16), values, preferred_element_type=F32) / total)
        mix = mixed[0] - lam * mixed[1]
        mix = mix * lax.rsqrt(jnp.mean(mix * mix, axis=1, keepdims=True) + 1e-05)
        mix = mix * gain_ref[...] * (1.0 - LAMBDA_BASE)
        attn[:, pl.ds(pl.multiple_of(h * wide, 128), wide)] = mix.astype(BF16)
        run_events(h, mid_events, end_events)
        return carry

    lax.fori_loop(0, heads, head_step, 0)

    split(
        lambda: (f_pass(2, 1), f_pass(2, 2)),
        lambda: f_pass(0, 3),
    )
    for k in range(4):
        o_shared(k)

    tile = 2 * half

    def project(n, carry):
        lanes = pl.ds(pl.multiple_of(n * tile, 128), tile)
        weight = wo[:, :, :, lanes].reshape(width, tile)
        value = jnp.dot(attn[...], weight, preferred_element_type=F32)
        stream[:, lanes] = (residual_ref[:, lanes].astype(F32) + value).astype(BF16)
        return carry

    lax.fori_loop(0, width // tile, project, 0)
    stream_f = stream[...].astype(F32)
    squares = jnp.mean(stream_f * stream_f, axis=1, keepdims=True)
    normed[quarter] = (stream_f * lax.rsqrt(squares + 1e-05) * norm_ref[...]).astype(BF16)

    def n_copy(q_from, i, device):
        block = normed.at[q_from]
        return send(block, block, n_send.at[i], n_recv.at[i], device)

    n_copy(quarter, 0, at_x).start()
    n_copy(quarter, 1, at_core).start()
    def relay():
        n_copy(q_x, 0, at_x).wait_recv()
        n_copy(q_x, 2, at_core).start()

    split(
        lambda: f_pass(2, 3),
        lambda: (f_pass(1, 2), f_pass(1, 3), f_pass(2, 1)),
    )
    for m in range(2):
        for k in range(4):
            f_y_recv(m, k)

    feed_events = {1: lambda: f_pass(2, 2), 3: lambda: f_pass(2, 3)}

    def feed(i, carry):
        run_events(i, {}, feed_events)

        @pl.when(i == 1)
        def _():
            n_copy(q_core, 1, at_core).wait_recv()

        @pl.when(i == 2)
        def _():
            relay()

        @pl.when(i == 3)
        def _():
            n_copy(q_diag, 2, at_core).wait_recv()

        slot = base_slot(i)
        tokens = normed[slot]

        def hidden_tile(n, inner_carry):
            lanes = pl.ds(pl.multiple_of(n * tile, 128), tile)
            gate = jnp.dot(tokens, wg[:, :, lanes].reshape(width, tile), preferred_element_type=F32)
            up = jnp.dot(tokens, wu[:, :, lanes].reshape(width, tile), preferred_element_type=F32)
            hidden[slot, :, lanes] = (gate / (1.0 + jnp.exp(-gate)) * up).astype(BF16)
            return inner_carry

        lax.fori_loop(0, units // tile, hidden_tile, 0)
        return carry

    def base_slot(i):
        q = (quarter + 2 * (i // 2)) % 4
        flip = i % 2
        return q + flip * (1 - 2 * (q % 2))

    lax.fori_loop(0, 4, feed, 0)

    def place(j):
        return order(j // 2) * 2 + (y + j) % 2

    def d_copy(i, p):
        if i == 0:
            return send(part.at[q_diag, p], got_core.at[0, p], d_send.at[0, p], d_recv.at[0, p], at_core)
        if i == 1:
            return send(part.at[q_core, p], got_core.at[1, p], d_send.at[1, p], d_recv.at[1, p], at_core)
        return send(to_x.at[p], got_x.at[p], d_send.at[2, p], d_recv.at[2, p], at_x)

    def d_sum(j):
        p = place(j)
        d_copy(0, p).wait_recv()
        to_x[p] = (part[q_x, p].astype(F32) + got_core[0, p].astype(F32)).astype(BF16)
        d_copy(2, p).start()

    def d_done(j):
        p = place(j)
        d_copy(1, p).wait_recv()
        d_copy(2, p).wait_recv()
        lanes = pl.ds(pl.multiple_of(p * rows, 128), rows)
        total = part[quarter, p].astype(F32) + got_core[1, p].astype(F32) + got_x[p].astype(F32)
        result_ref[:, lanes] = (stream[:, lanes].astype(F32) + total).astype(BF16)

    def down(j, carry):
        p = place(j)

        @pl.when(j % 2 == 1)
        def _():
            f_y_recv(2, j // 2)

        value = lax.dot_general(
            hidden[...].reshape(4 * rows, units), wd[p], (((1,), (1,)), ((), ())),
            preferred_element_type=F32,
        )
        value = value.astype(BF16).reshape(4, rows, value.shape[1])
        for g in range(4):
            part[g, p] = value[g]
        d_copy(0, p).start()
        d_copy(1, p).start()

        @pl.when(j >= 1)
        def _():
            d_sum(j - 1)

        @pl.when(j >= 2)
        def _():
            d_done(j - 2)

        return carry

    lax.fori_loop(0, 8, down, 0)
    d_sum(7)
    d_done(6)
    d_done(7)

    o_core.wait_send()
    o_y().wait_send()
    for group in firsts:
        for copy in group:
            copy.wait_send()
    for k in range(4):
        for s in range(2):
            z_wait_send(o_z(k, s))
        o_x(k).wait_send()
        o_c(k).wait_send()
        for m in range(3):
            for cut in range(2):
                z_wait_send(f_z(m, k, cut))
                f_y(m, k, cut).wait_send()
    n_copy(quarter, 0, at_x).wait_send()
    n_copy(quarter, 1, at_core).wait_send()
    n_copy(q_x, 2, at_core).wait_send()

    def drain(p, carry):
        for i in range(3):
            d_copy(i, p).wait_send()
        return carry

    lax.fori_loop(0, 8, drain, 0)


def per_device_kernel(
    queries, new_kv, cache_pool, page_table, assignment, lengths, lambda_vectors, subln_gain,
    residual, out_weight, norm_gain, gate_weight, up_weight, down_weight_t,
):
    rows, heads, wide = queries.shape
    pages, page_len = cache_pool.shape[:2]
    width, units = residual.shape[1], gate_weight.shape[1] // 4
    keys = pages * page_len + rows
    anyspace = pl.BlockSpec(memory_space=pl.ANY)
    vmem = pl.BlockSpec(memory_space=pltpu.VMEM)
    dma = pltpu.SemaphoreType.DMA
    return pl.pallas_call(
        layer_kernel,
        out_shape=jax.ShapeDtypeStruct((rows, width), BF16),
        in_specs=[pl.BlockSpec(memory_space=pltpu.SMEM)] * 3 + [vmem] * 4 + [anyspace] * 7,
        out_specs=vmem,
        scratch_shapes=[
            pltpu.VMEM((rows, heads, wide), BF16),
            pltpu.VMEM((keys // page_len, page_len, heads, 2 * wide), BF16),
            pltpu.VMEM((heads, rows, wide), BF16),
            pltpu.VMEM((heads, keys, 2 * wide), BF16),
            pltpu.VMEM((rows, width), BF16),
            pltpu.VMEM((4, 2, 256, width), BF16),
            pltpu.VMEM((8, 256, units), BF16),
            pltpu.VMEM((8, 256, units), BF16),
            pltpu.VMEM((8, 256, units), BF16),
            pltpu.VMEM((4, rows, width), BF16),
            pltpu.VMEM((rows, width), BF16),
            pltpu.VMEM((4, rows, units), BF16),
            pltpu.VMEM((4, 8, rows, 256), BF16),
            pltpu.VMEM((2, 8, rows, 256), BF16),
            pltpu.VMEM((8, rows, 256), BF16),
            pltpu.VMEM((8, rows, 256), BF16),
            dma((keys // page_len + 1,)), dma((4,)), dma((3, 3)), dma((3, 3)), dma((3, 2, 10)), dma((3, 2, 10)),
            dma((2, 6)), dma((2, 6)),
            dma((16,)), dma((16,)), dma((3,)), dma((3,)), dma((3, 8)), dma((3, 8)),
        ],
        compiler_params=pltpu.CompilerParams(
            collective_id=0, has_side_effects=True, vmem_limit_bytes=62 * 2**20
        ),
        name="layer",
    )(
        page_table, assignment, lengths, lambda_vectors, subln_gain.reshape(1, -1),
        norm_gain.reshape(1, -1), residual, queries, new_kv, cache_pool,
        out_weight, gate_weight, up_weight, down_weight_t,
    )


def solution(mesh):
    in_specs = (
        P("req", "mlp", None),
        P("req", "mlp", None),
        P("req", None, "mlp", None),
        P("req", None),
        P("req"),
        P(),
        P(),
        P(),
        P("req", "mlp"),
        P("req", "mlp"),
        P(),
        P("req", "mlp"),
        P("req", "mlp"),
        P("req", "mlp"),
    )
    out_specs = P("req", "mlp")
    small = mesh.shape["req"] == 32 and mesh.shape["mlp"] == 1
    return jax.shard_map(
        per_device_kernel if small else per_device, mesh=mesh, in_specs=in_specs, out_specs=out_specs, check_vma=False
    )
```
